512 devices in a mesh: seq: 64 (over z, x), head: 8 (over y, core).
Axes of the slice: x: 4, y: 4, z: 16, core: 2. Of those that a mesh axis runs over, the one named last changes fastest.
Arguments:
- queries: bfloat16 [32768, 3072], P(('seq', 'head')), may hold values from -48 to 48
- keys: bfloat16 [32768, 3072], P(('seq', 'head')), may hold values from -48 to 48
- values: bfloat16 [32768, 3072], P(('seq', 'head')), may hold values from -6 to 6
- tile_mask: int32 [256, 256], P('seq'), may hold values from 0 to 1, as said below
Outputs:
- attended: bfloat16 [32768, 3072], P(('seq', 'head'))
The draws below stay inside these ranges and needn't reach their ends.
Inputs may be any that keep to these rules, and one draw needn't show every extreme that they name: `tile_mask`: A query tile keeps only key tiles whose column, row and frame-tile each differ from its own by at most one; it always keeps its own tile, and the one tile whose column, row and frame-tile are all one more than its own (and the one whose three are all one less), where that tile exists.
All inputs are finite; a program needn't handle non-finite values.
Results may differ from the reference program's by a relative error of at most 0.0046.
Values may be sent and summed in bfloat16 or wider, within the bound.
A program may use at most 64 MiB of HBM per device.

```python
import math
import jax
import jax.numpy as jnp
import numpy as np
from jax import lax

HEADS = 24
HEAD_DIM = 128
TILE = 128
TILE_DEV = 4
TILE_H = 4
TILES = 256
TOKENS = 32768


def key_rows(key):
    return jax.random.normal(jax.random.fold_in(key, 11), (TOKENS, HEADS * HEAD_DIM), jnp.float32)


def draw_keys(key, part):
    base = key_rows(key)
    return base.astype(jnp.bfloat16)


def draw_queries(key, part):
    key = jax.random.fold_in(key, 5)
    own = jax.random.normal(key, (TOKENS, HEADS * HEAD_DIM), jnp.float32)
    return own.astype(jnp.bfloat16)


def draw_tile_mask(key, part):
    key = jax.random.fold_in(key, 7)
    index = jnp.arange(TILES, dtype=jnp.int32)
    shard = index // TILE_DEV
    column = index % TILE_DEV
    row = shard % TILE_H
    frame = shard // TILE_H
    d_col = column[None, :] - column[:, None]
    d_row = row[None, :] - row[:, None]
    d_frame = frame[None, :] - frame[:, None]
    window = (jnp.abs(d_col) <= 1) & (jnp.abs(d_row) <= 1) & (jnp.abs(d_frame) <= 1)
    same = (d_col == 0) & (d_row == 0) & (d_frame == 0)
    ahead = (d_col == 1) & (d_row == 1) & (d_frame == 1)
    behind = (d_col == -1) & (d_row == -1) & (d_frame == -1)
    coin = jax.random.randint(key, (TILES, TILES), 0, 2)
    kept = window & ((coin == 1) | same | ahead | behind)
    return kept.astype(jnp.int32)


def steps_of(key, extent, shards, low, largest):
    gain, own = 1.0, jax.random.fold_in(key, 6)
    for dim, blocks in shards:
        steps = jnp.exp(jax.random.uniform(jax.random.fold_in(own, dim), (blocks,), jnp.float32, low / len(shards), largest / len(shards)))
        gain = gain * jnp.repeat(steps, extent[dim] // blocks).reshape([-1 if axis == dim else 1 for axis in range(len(extent))])
    return gain


def centred(key, extent, deviation, most, split=(), kind=jnp.bfloat16):
    values = deviation * jax.random.normal(key, extent, jnp.float32)
    if split:
        values = values * steps_of(key, extent, split, -0.22, 0.18)
    return jnp.clip(values, -most, most).astype(kind)


def setup_inputs(seed: int = 0) -> dict:
    streams_of = jax.random.split(jax.random.key(seed), 5)
    return {
        "queries": draw_queries(jax.random.fold_in(streams_of[4], 71), 0),
        "keys": draw_keys(jax.random.fold_in(streams_of[4], 71), 0),
        "values": centred(streams_of[2], (TOKENS, HEADS * HEAD_DIM), 1.0, 6.0, ((0, 512),)),
        "tile_mask": draw_tile_mask(jax.random.fold_in(streams_of[4], 71), 0),
    }


def reference(queries, keys, values, tile_mask):
    frames = TILES // (TILE_DEV * TILE_H)
    q_tiles = queries.reshape(TILES, TILE, HEADS, HEAD_DIM)
    k_tiles = keys.reshape(TILES, TILE, HEADS, HEAD_DIM)
    v_tiles = values.reshape(TILES, TILE, HEADS, HEAD_DIM)
    scale = 1.0 / math.sqrt(HEAD_DIM)
    table = np.array([(a, b, c) for a in (-1, 0, 1) for b in (-1, 0, 1) for c in (-1, 0, 1)], dtype=np.int32)
    offsets = jnp.asarray(table)
    count = table.shape[0]

    def one_tile(index):
        column = index % TILE_DEV
        row = index // TILE_DEV % TILE_H
        frame = index // (TILE_DEV * TILE_H)
        fr = frame + offsets[:, 0]
        rw = row + offsets[:, 1]
        cl = column + offsets[:, 2]
        inside = (fr >= 0) & (fr < frames) & (rw >= 0) & (rw < TILE_H) & (cl >= 0) & (cl < TILE_DEV)
        other = jnp.clip((fr * TILE_H + rw) * TILE_DEV + cl, 0, TILES - 1).astype(jnp.int32)
        flags = tile_mask[index][other]
        kept = (flags > 0) & inside
        query = q_tiles[index].astype(jnp.float32)
        key_block = k_tiles[other].reshape(count * TILE, HEADS, HEAD_DIM).astype(jnp.float32)
        value_block = v_tiles[other].reshape(count * TILE, HEADS, HEAD_DIM).astype(jnp.float32)
        scores = jnp.einsum('qhd,khd->hqk', query, key_block) * scale
        wide = jnp.repeat(kept, TILE)[None, None, :]
        scores = jnp.where(wide, scores, -jnp.inf)
        top = lax.optimization_barrier(jnp.max(scores, axis=2, keepdims=True))
        weights = jnp.exp(scores - top)
        total = lax.optimization_barrier(jnp.sum(weights, axis=2, keepdims=True))
        probs = lax.optimization_barrier(weights.astype(jnp.bfloat16)).astype(jnp.float32)
        summed = jnp.einsum('hqk,khd->qhd', probs, value_block)
        result = summed / jnp.transpose(total, (1, 0, 2))
        return result.astype(jnp.bfloat16)
    tiles_out = lax.map(one_tile, jnp.arange(TILES, dtype=jnp.int32))
    return tiles_out.reshape(TOKENS, HEADS * HEAD_DIM)
```

```python
import math

import jax
import jax.numpy as jnp
from jax import lax
from jax.experimental import pallas as pl
from jax.experimental.pallas import tpu as pltpu
from jax.sharding import PartitionSpec as P

MESH = pl.DeviceIdType.MESH
BF16, F32 = jnp.bfloat16, jnp.float32
FRAMES, ROWS, COLS = 16, 4, 4
TILE, HALF, DIM = 128, 64, 128
GROUPS = 6
MASKED = -1e30


def kernel(q_ref, k_ref, v_ref, mask_ref, out_ref, kv, qb, mb, bias, scores, probs, top, total, acc, ob,
           recv_in, recv_z, recv_x, recv_q, recv_mask, recv_out,
           send_k, send_v, send_q, send_mask, send_z, send_x, send_out):
    seq, head = lax.axis_index("seq"), lax.axis_index("head")
    z, x = seq // ROWS, seq % ROWS
    y, c = head // 2, head % 2
    p, pair = y % 2, 2 * x + y // 2

    barrier = pltpu.get_barrier_semaphore()
    own = x * 8 + head

    def greet(k, carry):
        other = (own + k) % 32
        pl.semaphore_signal(barrier, inc=1, device_id=(z * ROWS + other // 8, other % 8), device_id_type=MESH)
        return carry

    lax.fori_loop(1, 32, greet, 0)
    above = ((z + 1) % FRAMES) * ROWS + x
    below = ((z + FRAMES - 1) % FRAMES) * ROWS + x
    for there in (above, below):
        pl.semaphore_signal(barrier, inc=1, device_id=(there, head), device_id_type=MESH)
    pl.semaphore_wait(barrier, 33)

    row_there = jnp.where(x < 2, x, 3 - x)
    core_there = x // 2
    near = jnp.where(y < 2, y, 3 - y)

    def target(phase, j):
        p_t = (y // 2 + phase) % 2
        x_t = (x + j) % 4
        yh_t = (y // 2 + j // 4) % 2
        y_t = 2 * yh_t + p_t
        w_t = 2 * x_t + yh_t
        col = near if phase == 0 else 3 - near
        here = (x_t == x) & (y_t == y) & (core_there == c)
        return (z * ROWS + x_t, 2 * y_t + core_there), 3 * w_t + 2 * p_t, 3 * w_t + 1, col, here

    def part(ref, h):
        return ref.at[:, pl.ds(pl.multiple_of(h * DIM, DIM), DIM)]

    def move(src, dst, send_sem, recv_sem, device, here, start):
        remote = pltpu.make_async_remote_copy(
            src_ref=src, dst_ref=dst, send_sem=send_sem, recv_sem=recv_sem, device_id=device, device_id_type=MESH
        )
        if start:
            @pl.when(here)
            def _():
                pltpu.make_async_copy(src, dst, recv_sem).start()

        @pl.when(jnp.logical_not(here))
        def _():
            if start:
                remote.start()
            else:
                remote.wait_send()

    def move_kv(phase, start):
        def body(j, carry):
            device, full, half, col, here = target(phase, j)
            sem = recv_in.at[row_there, col]
            for i, (ref, send) in enumerate(((k_ref, send_k), (v_ref, send_v))):
                move(part(ref, full), kv.at[1, row_there, col, 0, i, c], send.at[phase, j, 0], sem, device, here, start)

            def halves():
                for i, (ref, send) in enumerate(((k_ref, send_k), (v_ref, send_v))):
                    move(part(ref, half), kv.at[1, row_there, col, 1, i, c], send.at[phase, j, 1], sem, device, here, start)

            if phase == 0:
                halves()
            else:
                pl.when(near == 1)(halves)
            return carry

        lax.fori_loop(0, 8, body, 0)

    def move_q(phase, start):
        def body(j, carry):
            device, full, half, col, here = target(phase, j)
            move(part(q_ref, full), qb.at[col, row_there, c], send_q.at[phase, j, 0], recv_q.at[0], device, here, start)
            if phase == 0:
                move(part(q_ref, half), qb.at[4 + col, row_there, c], send_q.at[phase, j, 1], recv_q.at[0], device, here, start)
            return carry

        lax.fori_loop(0, 8, body, 0)

    def move_mask(start):
        for j in range(2):
            x_t = 2 * c + j
            here = (x_t == x) & (core_there == c)
            move(mask_ref, mb.at[row_there], send_mask.at[j], recv_mask.at[0],
                 (z * ROWS + x_t, 2 * y + core_there), here, start)

    move_kv(0, True)
    move_kv(1, True)
    move_mask(True)
    move_q(0, True)
    move_q(1, True)

    def chunk(slot, row, col):
        return kv.at[slot, row, col] if col < 3 else kv.at[slot, row, col, 0]

    def wait_for(ref, sem):
        pltpu.make_async_copy(ref, ref, sem).wait()

    def pass_on(row, col):
        return [
            pltpu.make_async_remote_copy(
                src_ref=chunk(1, row, col), dst_ref=chunk(slot, row, col),
                send_sem=send_z.at[slot // 2, row, col], recv_sem=recv_z.at[slot // 2, row, col],
                device_id=(there, head), device_id_type=MESH,
            )
            for slot, there in ((0, above), (2, below))
        ]

    def across(slot, col):
        return pltpu.make_async_remote_copy(
            src_ref=chunk(slot, 1, col), dst_ref=chunk(slot, 2, col),
            send_sem=send_x.at[slot, col], recv_sem=recv_x.at[slot, col],
            device_id=(seq, 2 * y + 1 - c), device_id_type=MESH,
        )

    for cols in ((0, 1), (2, 3)):
        for row in (1, 0):
            for col in cols:
                wait_for(chunk(1, row, col), recv_in.at[row, col])
                for copy in pass_on(row, col):
                    copy.start()
                if row == 1:
                    across(1, col).start()

    wait_for(mb, recv_mask.at[0])
    flags = mb[...]
    kept = jnp.where(flags > 0, 1.0, 0.0).astype(F32)
    forward = [kept[r, i:i + 1, :] for r in range(2) for i in range(4)]
    backward = [kept[r, 3 - i:4 - i, :] for r in range(2) for i in range(4)]
    forward, backward = jnp.concatenate(forward, axis=0), jnp.concatenate(backward, axis=0)
    kept = jnp.where(p == 0, forward, backward).astype(BF16)
    lane = lax.broadcasted_iota(jnp.int32, (256, 128), 1)
    tile = lax.broadcasted_iota(jnp.int32, (256, 128), 0)
    slot_of = jnp.where(lane >= 12, 1, 0) + jnp.where(lane >= 24, 1, 0)
    rest = lane - 12 * slot_of
    row_of, col_of = lax.shift_right_logical(rest, 2), lax.bitwise_and(rest, 3)
    row_of = jnp.where(c == 0, row_of, 3 - row_of)
    col_of = jnp.where(p == 0, col_of, 3 - col_of)
    wanted = ((z + slot_of - 1) * ROWS + row_of) * COLS + col_of
    select = jnp.where((wanted == tile) & (lane < 36), 1.0, 0.0).astype(BF16)
    picked = jnp.dot(kept, select, preferred_element_type=F32)
    offset = jnp.where(picked > 0.5, 0.0, MASKED)
    for i in range(36):
        bias[:, i * 128:(i + 1) * 128] = jnp.broadcast_to(offset[:, i:i + 1], (8, 128))

    wait_for(qb, recv_q.at[0])
    factor = math.log2(math.e) / math.sqrt(DIM)

    def attend(g, slots, first):
        hd, mid = (0, g) if g < 4 else (1, g - 4)
        lo, hi = max(0, mid - 1), min(3, mid + 1)
        n = hi - lo + 1
        blocks = [(slot, row) for slot in slots for row in range(3)]
        query = qb[g].reshape(2 * TILE, DIM)
        best = [None, None]
        for b, (slot, row) in enumerate(blocks):
            r0 = 0 if row < 2 else 1
            keys = kv[slot, row, lo:hi + 1, hd, 0].reshape(n * TILE, DIM)
            s = lax.dot_general(query[r0 * TILE:], keys, (((1,), (1,)), ((), ())), preferred_element_type=F32)
            for r in range(r0, 2):
                for t in range(n):
                    lanes = (slot * 12 + row * 4 + lo + t) * 128
                    piece = s[(r - r0) * TILE:(r - r0 + 1) * TILE, t * 128:(t + 1) * 128] * factor
                    piece = piece + bias[r * 4 + mid:r * 4 + mid + 1, lanes:lanes + 128]
                    scores[r, b * n + t] = piece
                    best[r] = piece if best[r] is None else jnp.maximum(best[r], piece)
        for r in range(2):
            highest = jnp.broadcast_to(jnp.max(best[r], axis=1, keepdims=True), (TILE, 128))
            if first:
                now, sums = highest, jnp.zeros((TILE, 128), F32)
            else:
                before = top[g, r]
                now = jnp.maximum(before, highest)
                shrink = jnp.exp2(before - now)
                sums = total[g, r] * shrink
                acc[g, r] = acc[g, r] * shrink
            for b, (slot, row) in enumerate(blocks):
                if row == 2 and r == 0:
                    continue
                for t in range(n):
                    weight = jnp.exp2(scores[r, b * n + t] - now)
                    sums = sums + weight
                    probs[r * TILE:(r + 1) * TILE, (b * n + t) * 128:(b * n + t + 1) * 128] = weight.astype(BF16)
            top[g, r], total[g, r] = now, sums
        result = [None, None]
        for b, (slot, row) in enumerate(blocks):
            r0 = 0 if row < 2 else 1
            vals = kv[slot, row, lo:hi + 1, hd, 1].reshape(n * TILE, DIM)
            o = jnp.dot(probs[r0 * TILE:, b * n * 128:(b + 1) * n * 128], vals, preferred_element_type=F32)
            for r in range(r0, 2):
                add = o[(r - r0) * TILE:(r - r0 + 1) * TILE]
                result[r] = add if result[r] is None else result[r] + add
        for r in range(2):
            acc[g, r] = result[r] if first else acc[g, r] + result[r]

    def bring(cols):
        for col in cols:
            for i, slot in enumerate((0, 2)):
                wait_for(chunk(slot, 1, col), recv_z.at[i, 1, col])
                across(slot, col).start()

    for cols, groups in (((0, 1), (0, 4)), ((2,), (1, 5)), ((3,), (2, 3))):
        for col in cols:
            wait_for(chunk(1, 2, col), recv_x.at[1, col])
        for g in groups:
            attend(g, (1,), True)
        if cols[0] > 0:
            bring((0, 1) if cols == (2,) else (2, 3))

    def send_back(g, start):
        hd, mid = (0, g) if g < 4 else (1, g - 4)
        y_t = jnp.where(p == 0, mid, 3 - mid)
        h = 3 * pair + (2 * p if hd == 0 else 1)
        for r in range(2):
            x_t = jnp.where(c == 0, r, 3 - r)
            for half in range(2):
                here = (x_t == x) & (y_t == y) & (c == half)
                move(ob.at[g, r, half], part(out_ref, h), send_out.at[g, r, half], recv_out.at[0],
                     (z * ROWS + x_t, 2 * y_t + half), here, start)

    for cols, groups in (((0, 1), (0, 4)), ((2,), (1, 5)), ((3,), (2, 3))):
        for col in cols:
            for i, slot in enumerate((0, 2)):
                wait_for(chunk(slot, 0, col), recv_z.at[i, 0, col])
                wait_for(chunk(slot, 2, col), recv_x.at[slot, col])
        for g in groups:
            attend(g, (0, 2), False)
            for r in range(2):
                whole = jnp.sum(total[g, r], axis=1, keepdims=True)
                ob[g, r] = (acc[g, r] / whole).astype(BF16).reshape(2, HALF, DIM)
            send_back(g, True)

    wait_for(out_ref, recv_out.at[0])
    move_kv(0, False)
    move_kv(1, False)
    move_mask(False)
    move_q(0, False)
    move_q(1, False)
    for col in range(4):
        for row in range(2):
            for copy in pass_on(row, col):
                copy.wait_send()
        for slot in range(3):
            across(slot, col).wait_send()
    for g in range(GROUPS):
        send_back(g, False)


def body(queries, keys, values, tile_mask):
    dma = pltpu.SemaphoreType.DMA
    return pl.pallas_call(
        kernel,
        out_shape=jax.ShapeDtypeStruct(queries.shape, BF16),
        in_specs=[pl.BlockSpec(memory_space=pl.ANY)] * 4,
        out_specs=pl.BlockSpec(memory_space=pl.ANY),
        scratch_shapes=[
            pltpu.VMEM((3, 3, 4, 2, 2, 2, HALF, DIM), BF16),
            pltpu.VMEM((GROUPS, 2, 2, HALF, DIM), BF16),
            pltpu.VMEM((2, 4, 256), jnp.int32),
            pltpu.VMEM((8, 36 * 128), F32),
            pltpu.VMEM((2, 18, TILE, 128), F32),
            pltpu.VMEM((2 * TILE, 18 * 128), BF16),
            pltpu.VMEM((GROUPS, 2, TILE, 128), F32),
            pltpu.VMEM((GROUPS, 2, TILE, 128), F32),
            pltpu.VMEM((GROUPS, 2, TILE, DIM), F32),
            pltpu.VMEM((GROUPS, 2, 2, HALF, DIM), BF16),
            dma((2, 4)), dma((2, 2, 4)), dma((3, 4)), dma((1,)), dma((1,)), dma((1,)),
            dma((2, 8, 2)), dma((2, 8, 2)), dma((2, 8, 2)), dma((2,)), dma((2, 2, 4)), dma((3, 4)), dma((GROUPS, 2, 2)),
        ],
        compiler_params=pltpu.CompilerParams(
            collective_id=0, has_side_effects=True, vmem_limit_bytes=48 * 1024 * 1024
        ),
        cost_estimate=pl.CostEstimate(flops=2_000_000_000, bytes_accessed=8_000_000, transcendentals=4_000_000),
    )(queries, keys, values, tile_mask)


def solution(mesh):
    placed = (
        P(("seq", "head"), None),
        P(("seq", "head"), None),
        P(("seq", "head"), None),
        P("seq", None),
    )
    return jax.shard_map(
        body, mesh=mesh, in_specs=placed, out_specs=P(("seq", "head"), None), check_vma=False
    )
```

```python
import math

import jax
import jax.numpy as jnp
from jax import lax
from jax.experimental import pallas as pl
from jax.experimental.pallas import tpu as pltpu
from jax.sharding import PartitionSpec as P

MESH = pl.DeviceIdType.MESH
BF16, F32 = jnp.bfloat16, jnp.float32
FRAMES, ROWS, COLS = 16, 4, 4
TILE, HALF, DIM = 128, 64, 128
GROUPS = 6
MASKED = -1e30


def kernel(q_ref, k_ref, v_ref, mask_ref, out_ref, kv, qb, mb, bias, scores, probs, top, total, acc, ob,
           recv_in, recv_z, recv_x, recv_q, recv_mask, recv_out,
           send_k, send_v, send_q, send_mask, send_z, send_x, send_out):
    seq, head = lax.axis_index("seq"), lax.axis_index("head")
    z, x = seq // ROWS, seq % ROWS
    y, c = head // 2, head % 2
    p, pair = y // 2, 2 * x + y % 2

    barrier = pltpu.get_barrier_semaphore()
    own = x * 8 + head

    def greet(k, carry):
        other = (own + k) % 32
        pl.semaphore_signal(barrier, inc=1, device_id=(z * ROWS + other // 8, other % 8), device_id_type=MESH)
        return carry

    lax.fori_loop(1, 32, greet, 0)
    above = ((z + 1) % FRAMES) * ROWS + x
    below = ((z + FRAMES - 1) % FRAMES) * ROWS + x
    for there in (above, below):
        pl.semaphore_signal(barrier, inc=1, device_id=(there, head), device_id_type=MESH)
    pl.semaphore_wait(barrier, 33)

    row_there = jnp.where(x < 2, x, 3 - x)
    core_there = x // 2
    near = jnp.where(y < 2, y, 3 - y)

    def target(phase, j):
        p_t = (y // 2 + phase) % 2
        x_t = (x + j // 2 + 2 * near) % 4
        yh_t = (y + c + j) % 2
        y_t = 2 * p_t + yh_t
        w_t = 2 * x_t + yh_t
        col = near if phase == 0 else 3 - near
        here = (x_t == x) & (y_t == y) & (core_there == c)
        return (z * ROWS + x_t, 2 * y_t + core_there), 3 * w_t + 2 * p_t, 3 * w_t + 1, col, here

    def part(ref, h):
        return ref.at[:, pl.ds(pl.multiple_of(h * DIM, DIM), DIM)]

    def move(src, dst, send_sem, recv_sem, device, here, start):
        remote = pltpu.make_async_remote_copy(
            src_ref=src, dst_ref=dst, send_sem=send_sem, recv_sem=recv_sem, device_id=device, device_id_type=MESH
        )
        if start:
            @pl.when(here)
            def _():
                pltpu.make_async_copy(src, dst, recv_sem).start()

        @pl.when(jnp.logical_not(here))
        def _():
            if start:
                remote.start()
            else:
                remote.wait_send()

    def move_kv(phase, start):
        def body(j, carry):
            device, full, half, col, here = target(phase, j)
            sem = recv_in.at[row_there, col]
            for i, (ref, send) in enumerate(((k_ref, send_k), (v_ref, send_v))):
                move(part(ref, full), kv.at[1, row_there, col, 0, i, c], send.at[phase, j, 0], sem, device, here, start)

            def halves():
                for i, (ref, send) in enumerate(((k_ref, send_k), (v_ref, send_v))):
                    move(part(ref, half), kv.at[1, row_there, col, 1, i, c], send.at[phase, j, 1], sem, device, here, start)

            if phase == 0:
                halves()
            else:
                pl.when(near == 1)(halves)
            return carry

        lax.fori_loop(0, 8, body, 0)

    def move_q(phase, start):
        def body(j, carry):
            device, full, half, col, here = target(phase, j)
            move(part(q_ref, full), qb.at[col, row_there, c], send_q.at[phase, j, 0], recv_q.at[0], device, here, start)
            if phase == 0:
                move(part(q_ref, half), qb.at[4 + col, row_there, c], send_q.at[phase, j, 1], recv_q.at[0], device, here, start)
            return carry

        lax.fori_loop(0, 8, body, 0)

    def move_mask(start):
        for j in range(2):
            x_t = 2 * c + j
            here = (x_t == x) & (core_there == c)
            move(mask_ref, mb.at[row_there], send_mask.at[j], recv_mask.at[0],
                 (z * ROWS + x_t, 2 * y + core_there), here, start)

    move_kv(0, True)
    move_kv(1, True)
    move_mask(True)
    move_q(0, True)
    move_q(1, True)

    def chunk(slot, row, col):
        return kv.at[slot, row, col, 0] if isinstance(col, int) and col == 3 else kv.at[slot, row, col]

    def wait_for(ref, sem):
        pltpu.make_async_copy(ref, ref, sem).wait()

    def pass_on(row, col):
        return [
            pltpu.make_async_remote_copy(
                src_ref=chunk(1, row, col), dst_ref=chunk(slot, row, col),
                send_sem=send_z.at[slot // 2, row, col], recv_sem=recv_z.at[slot // 2, row, col],
                device_id=(there, head), device_id_type=MESH,
            )
            for slot, there in ((0, above), (2, below))
        ]

    def across(slot, col):
        return pltpu.make_async_remote_copy(
            src_ref=chunk(slot, 1, col), dst_ref=chunk(slot, 2, col),
            send_sem=send_x.at[slot, col], recv_sem=recv_x.at[slot, col],
            device_id=(seq, 2 * y + 1 - c), device_id_type=MESH,
        )

    def forward(row, col):
        wait_for(chunk(1, row, col), recv_in.at[row, col])
        for copy in pass_on(row, col):
            copy.start()

    def forward_near(i, carry):
        gap = (x + 4 - i) % 4
        x_from = 2 * c + gap % 2
        col = ((gap + 4 - x_from) % 4) // 2
        row = jnp.where(c == 0, x_from, 3 - x_from)
        forward(row, col)

        @pl.when(row == 1)
        def _():
            across(1, col).start()

        return carry

    lax.fori_loop(0, 4, forward_near, 0)

    def forward_far(col):
        forward(1, col)
        across(1, col).start()
        forward(0, col)

    forward_far(2)
    forward_far(3)

    wait_for(mb, recv_mask.at[0])
    flags = mb[...]
    kept = jnp.where(flags > 0, 1.0, 0.0).astype(F32)
    ahead = [kept[r, i:i + 1, :] for r in range(2) for i in range(4)]
    back = [kept[r, 3 - i:4 - i, :] for r in range(2) for i in range(4)]
    ahead, back = jnp.concatenate(ahead, axis=0), jnp.concatenate(back, axis=0)
    kept = jnp.where(p == 0, ahead, back).astype(BF16)
    lane = lax.broadcasted_iota(jnp.int32, (256, 128), 1)
    tile = lax.broadcasted_iota(jnp.int32, (256, 128), 0)
    slot_of = jnp.where(lane >= 12, 1, 0) + jnp.where(lane >= 24, 1, 0)
    rest = lane - 12 * slot_of
    row_of, col_of = lax.shift_right_logical(rest, 2), lax.bitwise_and(rest, 3)
    row_of = jnp.where(c == 0, row_of, 3 - row_of)
    col_of = jnp.where(p == 0, col_of, 3 - col_of)
    wanted = ((z + slot_of - 1) * ROWS + row_of) * COLS + col_of
    select = jnp.where((wanted == tile) & (lane < 36), 1.0, 0.0).astype(BF16)
    picked = jnp.dot(kept, select, preferred_element_type=F32)
    offset = jnp.where(picked > 0.5, 0.0, MASKED)
    for i in range(36):
        bias[:, i * 128:(i + 1) * 128] = jnp.broadcast_to(offset[:, i:i + 1], (8, 128))

    wait_for(qb, recv_q.at[0])
    factor = math.log2(math.e) / math.sqrt(DIM)

    def attend(g, slots, first):
        hd, mid = (0, g) if g < 4 else (1, g - 4)
        lo, hi = max(0, mid - 1), min(3, mid + 1)
        n = hi - lo + 1
        blocks = [(slot, row) for slot in slots for row in range(3)]
        query = qb[g].reshape(2 * TILE, DIM)
        best = [None, None]
        for b, (slot, row) in enumerate(blocks):
            r0 = 0 if row < 2 else 1
            keys = kv[slot, row, lo:hi + 1, hd, 0].reshape(n * TILE, DIM)
            s = lax.dot_general(query[r0 * TILE:], keys, (((1,), (1,)), ((), ())), preferred_element_type=F32)
            for r in range(r0, 2):
                for t in range(n):
                    lanes = (slot * 12 + row * 4 + lo + t) * 128
                    piece = s[(r - r0) * TILE:(r - r0 + 1) * TILE, t * 128:(t + 1) * 128] * factor
                    piece = piece + bias[r * 4 + mid:r * 4 + mid + 1, lanes:lanes + 128]
                    scores[r, b * n + t] = piece
                    best[r] = piece if best[r] is None else jnp.maximum(best[r], piece)
        for r in range(2):
            highest = jnp.broadcast_to(jnp.max(best[r], axis=1, keepdims=True), (TILE, 128))
            if first:
                now, sums = highest, jnp.zeros((TILE, 128), F32)
            else:
                before = top[g, r]
                now = jnp.maximum(before, highest)
                shrink = jnp.exp2(before - now)
                sums = total[g, r] * shrink
                acc[g, r] = acc[g, r] * shrink
            for b, (slot, row) in enumerate(blocks):
                if row == 2 and r == 0:
                    continue
                for t in range(n):
                    weight = jnp.exp2(scores[r, b * n + t] - now)
                    sums = sums + weight
                    probs[r * TILE:(r + 1) * TILE, (b * n + t) * 128:(b * n + t + 1) * 128] = weight.astype(BF16)
            top[g, r], total[g, r] = now, sums
        result = [None, None]
        for b, (slot, row) in enumerate(blocks):
            r0 = 0 if row < 2 else 1
            vals = kv[slot, row, lo:hi + 1, hd, 1].reshape(n * TILE, DIM)
            o = jnp.dot(probs[r0 * TILE:, b * n * 128:(b + 1) * n * 128], vals, preferred_element_type=F32)
            for r in range(r0, 2):
                add = o[(r - r0) * TILE:(r - r0 + 1) * TILE]
                result[r] = add if result[r] is None else result[r] + add
        for r in range(2):
            acc[g, r] = result[r] if first else acc[g, r] + result[r]

    def bring(cols):
        for col in cols:
            for i, slot in enumerate((0, 2)):
                wait_for(chunk(slot, 1, col), recv_z.at[i, 1, col])
                across(slot, col).start()

    for col in (0, 1):
        wait_for(chunk(1, 2, col), recv_x.at[1, col])
    attend(0, (1,), True)
    attend(4, (1,), True)
    bring((0, 1))
    wait_for(chunk(1, 2, 2), recv_x.at[1, 2])
    for g in (1, 5):
        attend(g, (1,), True)
    wait_for(chunk(1, 2, 3), recv_x.at[1, 3])
    for g in (2, 3):
        attend(g, (1,), True)

    def send_back(g, start):
        hd, mid = (0, g) if g < 4 else (1, g - 4)
        y_t = jnp.where(p == 0, mid, 3 - mid)
        h = 3 * pair + (2 * p if hd == 0 else 1)
        for r in range(2):
            x_t = jnp.where(c == 0, r, 3 - r)
            for half in range(2):
                here = (x_t == x) & (y_t == y) & (c == half)
                move(ob.at[g, r, half], part(out_ref, h), send_out.at[g, r, half], recv_out.at[0],
                     (z * ROWS + x_t, 2 * y_t + half), here, start)

    for cols, groups in (((0, 1), (0, 4)), ((2,), (1, 5)), ((3,), (2, 3))):
        if cols[0] > 0:
            bring(cols)
        for col in cols:
            for i, slot in enumerate((0, 2)):
                wait_for(chunk(slot, 0, col), recv_z.at[i, 0, col])
                wait_for(chunk(slot, 2, col), recv_x.at[slot, col])
        for g in groups:
            attend(g, (0, 2), False)
            for r in range(2):
                whole = jnp.sum(total[g, r], axis=1, keepdims=True)
                ob[g, r] = (acc[g, r] / whole).astype(BF16).reshape(2, HALF, DIM)
            send_back(g, True)

    wait_for(out_ref, recv_out.at[0])
    move_kv(0, False)
    move_kv(1, False)
    move_mask(False)
    move_q(0, False)
    move_q(1, False)
    for col in range(4):
        for row in range(2):
            for copy in pass_on(row, col):
                copy.wait_send()
        for slot in range(3):
            across(slot, col).wait_send()
    for g in range(GROUPS):
        send_back(g, False)


def body(queries, keys, values, tile_mask):
    dma = pltpu.SemaphoreType.DMA
    return pl.pallas_call(
        kernel,
        out_shape=jax.ShapeDtypeStruct(queries.shape, BF16),
        in_specs=[pl.BlockSpec(memory_space=pl.ANY)] * 4,
        out_specs=pl.BlockSpec(memory_space=pl.ANY),
        scratch_shapes=[
            pltpu.VMEM((3, 3, 4, 2, 2, 2, HALF, DIM), BF16),
            pltpu.VMEM((GROUPS, 2, 2, HALF, DIM), BF16),
            pltpu.VMEM((2, 4, 256), jnp.int32),
            pltpu.VMEM((8, 36 * 128), F32),
            pltpu.VMEM((2, 18, TILE, 128), F32),
            pltpu.VMEM((2 * TILE, 18 * 128), BF16),
            pltpu.VMEM((GROUPS, 2, TILE, 128), F32),
            pltpu.VMEM((GROUPS, 2, TILE, 128), F32),
            pltpu.VMEM((GROUPS, 2, TILE, DIM), F32),
            pltpu.VMEM((GROUPS, 2, 2, HALF, DIM), BF16),
            dma((2, 4)), dma((2, 2, 4)), dma((3, 4)), dma((1,)), dma((1,)), dma((1,)),
            dma((2, 8, 2)), dma((2, 8, 2)), dma((2, 8, 2)), dma((2,)), dma((2, 2, 4)), dma((3, 4)), dma((GROUPS, 2, 2)),
        ],
        compiler_params=pltpu.CompilerParams(
            collective_id=0, has_side_effects=True, vmem_limit_bytes=62 * 1024 * 1024
        ),
        cost_estimate=pl.CostEstimate(flops=2_000_000_000, bytes_accessed=8_000_000, transcendentals=4_000_000),
    )(queries, keys, values, tile_mask)


def solution(mesh):
    placed = (
        P(("seq", "head"), None),
        P(("seq", "head"), None),
        P(("seq", "head"), None),
        P("seq", None),
    )
    return jax.shard_map(
        body, mesh=mesh, in_specs=placed, out_specs=P(("seq", "head"), None), check_vma=False
    )
```

```python
import math

import jax
import jax.numpy as jnp
from jax import lax
from jax.experimental import pallas as pl
from jax.experimental.pallas import tpu as pltpu
from jax.sharding import PartitionSpec as P

MESH = pl.DeviceIdType.MESH
BF16, F32 = jnp.bfloat16, jnp.float32
FRAMES, ROWS, COLS = 16, 4, 4
TILE, HALF, DIM = 128, 64, 128
GROUPS = 6
MASKED = -1e30


def kernel(q_ref, k_ref, v_ref, mask_ref, out_ref, kv, qb, mb, bias, scores, probs, top, total, acc, ob,
           recv_in, recv_z, recv_x, recv_q, recv_mask, recv_out,
           send_k, send_v, send_q, send_mask, send_z, send_x, send_out, entered):
    seq, head = lax.axis_index("seq"), lax.axis_index("head")
    z, x = seq // ROWS, seq % ROWS
    y, c = head // 2, head % 2
    p, pair = y // 2, 2 * x + y % 2

    barrier = pltpu.get_barrier_semaphore()
    own = x * 8 + head

    def greet(k, carry):
        other = (own + k) % 32
        pl.semaphore_signal(barrier, inc=1, device_id=(z * ROWS + other // 8, other % 8), device_id_type=MESH)
        return carry

    lax.fori_loop(1, 32, greet, 0)
    above, below = seq + ROWS, seq - ROWS
    has_above, has_below = z < FRAMES - 1, z > 0

    @pl.when(has_above)
    def _():
        pl.semaphore_signal(barrier, inc=1, device_id=(above, head), device_id_type=MESH)

    @pl.when(z > 1)
    def _():
        pl.semaphore_signal(barrier, inc=1, device_id=(below, head), device_id_type=MESH)

    pl.semaphore_wait(barrier, jnp.where(z == 0, 31, jnp.where(has_above, 33, 32)))

    @pl.when(z == 1)
    def _():
        pl.semaphore_signal(entered, inc=1, device_id=(below, head), device_id_type=MESH)

    for slot, has in ((0, has_below), (2, has_above)):
        @pl.when(jnp.logical_not(has))
        def _():
            kv[slot] = jnp.zeros_like(kv[slot])

    row_there = jnp.where(x < 2, x, 3 - x)
    core_there = x // 2
    near = jnp.where(y < 2, y, 3 - y)

    def target(phase, j):
        p_t = (y // 2 + phase) % 2
        x_t = (x + j // 2 + 2 * near) % 4
        yh_t = (y + c + j) % 2
        y_t = 2 * p_t + yh_t
        w_t = 2 * x_t + yh_t
        col = near if phase == 0 else 3 - near
        here = (x_t == x) & (y_t == y) & (core_there == c)
        return (z * ROWS + x_t, 2 * y_t + core_there), 3 * w_t + 2 * p_t, 3 * w_t + 1, col, here

    def part(ref, h):
        return ref.at[:, pl.ds(pl.multiple_of(h * DIM, DIM), DIM)]

    def move(src, dst, send_sem, recv_sem, device, here, start):
        remote = pltpu.make_async_remote_copy(
            src_ref=src, dst_ref=dst, send_sem=send_sem, recv_sem=recv_sem, device_id=device, device_id_type=MESH
        )
        if start:
            @pl.when(here)
            def _():
                pltpu.make_async_copy(src, dst, recv_sem).start()

        @pl.when(jnp.logical_not(here))
        def _():
            if start:
                remote.start()
            else:
                remote.wait_send()

    def move_kv(phase, start):
        def body(j, carry):
            device, full, half, col, here = target(phase, j)
            sem = recv_in.at[row_there, col]
            for i, (ref, send) in enumerate(((k_ref, send_k), (v_ref, send_v))):
                move(part(ref, full), kv.at[1, row_there, col, 0, i, c], send.at[phase, j, 0], sem, device, here, start)

            def halves():
                for i, (ref, send) in enumerate(((k_ref, send_k), (v_ref, send_v))):
                    move(part(ref, half), kv.at[1, row_there, col, 1, i, c], send.at[phase, j, 1], sem, device, here, start)

            if phase == 0:
                halves()
            else:
                pl.when(near == 1)(halves)
            return carry

        lax.fori_loop(0, 8, body, 0)

    def move_q(phase, start):
        def body(j, carry):
            device, full, half, col, here = target(phase, j)
            move(part(q_ref, full), qb.at[col, row_there, c], send_q.at[phase, j, 0], recv_q.at[0], device, here, start)
            if phase == 0:
                move(part(q_ref, half), qb.at[4 + col, row_there, c], send_q.at[phase, j, 1], recv_q.at[0], device, here, start)
            return carry

        lax.fori_loop(0, 8, body, 0)

    def move_mask(start):
        for j in range(2):
            x_t = 2 * c + j
            here = (x_t == x) & (core_there == c)
            move(mask_ref, mb.at[row_there], send_mask.at[j], recv_mask.at[0],
                 (z * ROWS + x_t, 2 * y + core_there), here, start)

    move_kv(0, True)
    move_kv(1, True)
    move_mask(True)

    def chunk(slot, row, col):
        return kv.at[slot, row, col, 0] if isinstance(col, int) and col == 3 else kv.at[slot, row, col]

    def wait_for(ref, sem):
        pltpu.make_async_copy(ref, ref, sem).wait()

    def pass_on(row, col):
        return [
            (has, pltpu.make_async_remote_copy(
                src_ref=chunk(1, row, col), dst_ref=chunk(slot, row, col),
                send_sem=send_z.at[slot // 2, row, col], recv_sem=recv_z.at[slot // 2, row, col],
                device_id=(there, head), device_id_type=MESH,
            ))
            for slot, there, has in ((0, above, has_above), (2, below, has_below))
        ]

    def across(slot, col):
        return pltpu.make_async_remote_copy(
            src_ref=chunk(slot, 1, col), dst_ref=chunk(slot, 2, col),
            send_sem=send_x.at[slot, col], recv_sem=recv_x.at[slot, col],
            device_id=(seq, 2 * y + 1 - c), device_id_type=MESH,
        )

    def forward(row, col):
        wait_for(chunk(1, row, col), recv_in.at[row, col])
        for has, copy in pass_on(row, col):
            pl.when(has)(copy.start)

    def forward_near(i, carry):
        gap = (x + 4 - i) % 4
        x_from = 2 * c + gap % 2
        col = ((gap + 4 - x_from) % 4) // 2
        row = jnp.where(c == 0, x_from, 3 - x_from)
        forward(row, col)

        @pl.when(row == 1)
        def _():
            across(1, col).start()

        return carry

    @pl.when(z == 0)
    def _():
        pl.semaphore_wait(entered, 1)

    lax.fori_loop(0, 4, forward_near, 0)
    move_q(0, True)
    move_q(1, True)

    def forward_far(col):
        forward(1, col)
        across(1, col).start()
        forward(0, col)

    forward_far(2)
    forward_far(3)

    wait_for(mb, recv_mask.at[0])
    flags = mb[...]
    kept = jnp.where(flags > 0, 1.0, 0.0).astype(F32)
    ahead = [kept[r, i:i + 1, :] for r in range(2) for i in range(4)]
    back = [kept[r, 3 - i:4 - i, :] for r in range(2) for i in range(4)]
    ahead, back = jnp.concatenate(ahead, axis=0), jnp.concatenate(back, axis=0)
    kept = jnp.where(p == 0, ahead, back).astype(BF16)
    lane = lax.broadcasted_iota(jnp.int32, (256, 128), 1)
    tile = lax.broadcasted_iota(jnp.int32, (256, 128), 0)
    slot_of = jnp.where(lane >= 12, 1, 0) + jnp.where(lane >= 24, 1, 0)
    rest = lane - 12 * slot_of
    row_of, col_of = lax.shift_right_logical(rest, 2), lax.bitwise_and(rest, 3)
    row_of = jnp.where(c == 0, row_of, 3 - row_of)
    col_of = jnp.where(p == 0, col_of, 3 - col_of)
    wanted = ((z + slot_of - 1) * ROWS + row_of) * COLS + col_of
    select = jnp.where((wanted == tile) & (lane < 36), 1.0, 0.0).astype(BF16)
    picked = jnp.dot(kept, select, preferred_element_type=F32)
    offset = jnp.where(picked > 0.5, 0.0, MASKED)
    for i in range(36):
        bias[:, i * 128:(i + 1) * 128] = jnp.broadcast_to(offset[:, i:i + 1], (8, 128))

    wait_for(qb, recv_q.at[0])
    factor = math.log2(math.e) / math.sqrt(DIM)

    def attend(g, slots, first):
        hd, mid = (0, g) if g < 4 else (1, g - 4)
        lo, hi = max(0, mid - 1), min(3, mid + 1)
        n = hi - lo + 1
        blocks = [(slot, row) for slot in slots for row in range(3)]
        query = qb[g].reshape(2 * TILE, DIM)
        best = [None, None]
        for b, (slot, row) in enumerate(blocks):
            r0 = 0 if row < 2 else 1
            keys = kv[slot, row, lo:hi + 1, hd, 0].reshape(n * TILE, DIM)
            s = lax.dot_general(query[r0 * TILE:], keys, (((1,), (1,)), ((), ())), preferred_element_type=F32)
            for r in range(r0, 2):
                for t in range(n):
                    lanes = (slot * 12 + row * 4 + lo + t) * 128
                    piece = s[(r - r0) * TILE:(r - r0 + 1) * TILE, t * 128:(t + 1) * 128] * factor
                    piece = piece + bias[r * 4 + mid:r * 4 + mid + 1, lanes:lanes + 128]
                    scores[r, b * n + t] = piece
                    best[r] = piece if best[r] is None else jnp.maximum(best[r], piece)
        for r in range(2):
            highest = jnp.broadcast_to(jnp.max(best[r], axis=1, keepdims=True), (TILE, 128))
            if first:
                now, sums = highest, jnp.zeros((TILE, 128), F32)
            else:
                before = top[g, r]
                now = jnp.maximum(before, highest)
                shrink = jnp.exp2(before - now)
                sums = total[g, r] * shrink
                acc[g, r] = acc[g, r] * shrink
            for b, (slot, row) in enumerate(blocks):
                if row == 2 and r == 0:
                    continue
                for t in range(n):
                    weight = jnp.exp2(scores[r, b * n + t] - now)
                    sums = sums + weight
                    probs[r * TILE:(r + 1) * TILE, (b * n + t) * 128:(b * n + t + 1) * 128] = weight.astype(BF16)
            top[g, r], total[g, r] = now, sums
        result = [None, None]
        for b, (slot, row) in enumerate(blocks):
            r0 = 0 if row < 2 else 1
            vals = kv[slot, row, lo:hi + 1, hd, 1].reshape(n * TILE, DIM)
            o = jnp.dot(probs[r0 * TILE:, b * n * 128:(b + 1) * n * 128], vals, preferred_element_type=F32)
            for r in range(r0, 2):
                add = o[(r - r0) * TILE:(r - r0 + 1) * TILE]
                result[r] = add if result[r] is None else result[r] + add
        for r in range(2):
            acc[g, r] = result[r] if first else acc[g, r] + result[r]

    def bring(cols):
        for col in cols:
            for i, (slot, has) in enumerate(((0, has_below), (2, has_above))):
                @pl.when(has)
                def _():
                    wait_for(chunk(slot, 1, col), recv_z.at[i, 1, col])
                    across(slot, col).start()

    for col in (0, 1):
        wait_for(chunk(1, 2, col), recv_x.at[1, col])
    attend(0, (1,), True)
    attend(4, (1,), True)
    bring((0, 1))
    wait_for(chunk(1, 2, 2), recv_x.at[1, 2])
    for g in (1, 5):
        attend(g, (1,), True)
    wait_for(chunk(1, 2, 3), recv_x.at[1, 3])
    for g in (2, 3):
        attend(g, (1,), True)

    def send_back(g, start):
        hd, mid = (0, g) if g < 4 else (1, g - 4)
        y_t = jnp.where(p == 0, mid, 3 - mid)
        h = 3 * pair + (2 * p if hd == 0 else 1)
        for r in range(2):
            x_t = jnp.where(c == 0, r, 3 - r)
            for half in range(2):
                here = (x_t == x) & (y_t == y) & (c == half)
                move(ob.at[g, r, half], part(out_ref, h), send_out.at[g, r, half], recv_out.at[0],
                     (z * ROWS + x_t, 2 * y_t + half), here, start)

    for cols, groups in (((0, 1), (0, 4)), ((2,), (1, 5)), ((3,), (2, 3))):
        if cols[0] > 0:
            bring(cols)
        for col in cols:
            for i, (slot, has) in enumerate(((0, has_below), (2, has_above))):
                @pl.when(has)
                def _():
                    wait_for(chunk(slot, 0, col), recv_z.at[i, 0, col])
                    wait_for(chunk(slot, 2, col), recv_x.at[slot, col])
        for g in groups:
            attend(g, (0, 2), False)
            for r in range(2):
                whole = jnp.sum(total[g, r], axis=1, keepdims=True)
                ob[g, r] = (acc[g, r] / whole).astype(BF16).reshape(2, HALF, DIM)
            send_back(g, True)

    wait_for(out_ref, recv_out.at[0])
    move_kv(0, False)
    move_kv(1, False)
    move_mask(False)
    move_q(0, False)
    move_q(1, False)
    for col in range(4):
        for row in range(2):
            for has, copy in pass_on(row, col):
                pl.when(has)(copy.wait_send)
        for slot, has in ((0, has_below), (1, None), (2, has_above)):
            copy = across(slot, col)
            if has is None:
                copy.wait_send()
            else:
                pl.when(has)(copy.wait_send)
    for g in range(GROUPS):
        send_back(g, False)


def body(queries, keys, values, tile_mask):
    dma = pltpu.SemaphoreType.DMA
    return pl.pallas_call(
        kernel,
        out_shape=jax.ShapeDtypeStruct(queries.shape, BF16),
        in_specs=[pl.BlockSpec(memory_space=pl.ANY)] * 4,
        out_specs=pl.BlockSpec(memory_space=pl.ANY),
        scratch_shapes=[
            pltpu.VMEM((3, 3, 4, 2, 2, 2, HALF, DIM), BF16),
            pltpu.VMEM((GROUPS, 2, 2, HALF, DIM), BF16),
            pltpu.VMEM((2, 4, 256), jnp.int32),
            pltpu.VMEM((8, 36 * 128), F32),
            pltpu.VMEM((2, 18, TILE, 128), F32),
            pltpu.VMEM((2 * TILE, 18 * 128), BF16),
            pltpu.VMEM((GROUPS, 2, TILE, 128), F32),
            pltpu.VMEM((GROUPS, 2, TILE, 128), F32),
            pltpu.VMEM((GROUPS, 2, TILE, DIM), F32),
            pltpu.VMEM((GROUPS, 2, 2, HALF, DIM), BF16),
            dma((2, 4)), dma((2, 2, 4)), dma((3, 4)), dma((1,)), dma((1,)), dma((1,)),
            dma((2, 8, 2)), dma((2, 8, 2)), dma((2, 8, 2)), dma((2,)), dma((2, 2, 4)), dma((3, 4)), dma((GROUPS, 2, 2)),
            pltpu.SemaphoreType.REGULAR,
        ],
        compiler_params=pltpu.CompilerParams(
            collective_id=0, has_side_effects=True, vmem_limit_bytes=62 * 1024 * 1024
        ),
        cost_estimate=pl.CostEstimate(flops=2_000_000_000, bytes_accessed=8_000_000, transcendentals=4_000_000),
    )(queries, keys, values, tile_mask)


def solution(mesh):
    placed = (
        P(("seq", "head"), None),
        P(("seq", "head"), None),
        P(("seq", "head"), None),
        P("seq", None),
    )
    return jax.shard_map(
        body, mesh=mesh, in_specs=placed, out_specs=P(("seq", "head"), None), check_vma=False
    )
```

```python
import math

import jax
import jax.numpy as jnp
from jax import lax
from jax.experimental import pallas as pl
from jax.experimental.pallas import tpu as pltpu
from jax.sharding import PartitionSpec as P

MESH = pl.DeviceIdType.MESH
BF16, F32 = jnp.bfloat16, jnp.float32
FRAMES, ROWS, COLS = 16, 4, 4
TILE, HALF, DIM = 128, 64, 128
GROUPS = 6
MASKED = -1e30
PLACE = (0, 1, 4, 5, 2, 3)


def kernel(q_ref, k_ref, v_ref, mask_ref, out_ref, kv, qb, mb, bias, scores, probs, top, total, acc, ob,
           recv_in, recv_z, recv_x, recv_q, recv_mask, recv_out,
           send_near, send_far, send_mask, send_z, send_x, send_out, entered,
           recv_lent, send_lent, recv_lent_x):
    seq, head = lax.axis_index("seq"), lax.axis_index("head")
    z, x = seq // ROWS, seq % ROWS
    y, c = head // 2, head % 2
    p, pair = y // 2, 2 * x + y % 2

    barrier = pltpu.get_barrier_semaphore()
    own = x * 8 + head

    def greet(k, carry):
        other = (own + k) % 32
        pl.semaphore_signal(barrier, inc=1, device_id=(z * ROWS + other // 8, other % 8), device_id_type=MESH)
        return carry

    lax.fori_loop(1, 32, greet, 0)
    above, below = seq + ROWS, seq - ROWS
    has_above, has_below = z < FRAMES - 1, z > 0

    @pl.when(has_above)
    def _():
        pl.semaphore_signal(barrier, inc=1, device_id=(above, head), device_id_type=MESH)

    @pl.when(z > 1)
    def _():
        pl.semaphore_signal(barrier, inc=1, device_id=(below, head), device_id_type=MESH)

    pl.semaphore_wait(barrier, jnp.where(z == 0, 31, jnp.where(has_above, 33, 32)))

    @pl.when(z == 1)
    def _():
        pl.semaphore_signal(entered, inc=1, device_id=(below, head), device_id_type=MESH)

    for slot, has in ((0, has_below), (2, has_above)):
        @pl.when(jnp.logical_not(has))
        def _():
            kv[slot] = jnp.zeros_like(kv[slot])

    row_there = jnp.where(x < 2, x, 3 - x)
    core_there = x // 2
    near = jnp.where(y < 2, y, 3 - y)

    def target(phase, j):
        p_t = (y // 2 + phase) % 2
        x_t = (x + j // 2 + 2 * near) % 4
        yh_t = (y + c + j) % 2
        y_t = 2 * p_t + yh_t
        w_t = 2 * x_t + yh_t
        col = near if phase == 0 else 3 - near
        here = (x_t == x) & (y_t == y) & (core_there == c) if phase == 0 else None
        return (z * ROWS + x_t, 2 * y_t + core_there), 3 * w_t + 2 * p_t, 3 * w_t + 1, col, here

    def part(ref, h):
        return ref.at[:, pl.ds(pl.multiple_of(h * DIM, DIM), DIM)]

    def wait_for(ref, sem):
        pltpu.make_async_copy(ref, ref, sem).wait()

    def move(src, dst, send_sem, recv_sem, device, here=None):
        remote = pltpu.make_async_remote_copy(
            src_ref=src, dst_ref=dst, send_sem=send_sem, recv_sem=recv_sem, device_id=device, device_id_type=MESH
        )
        if here is None:
            remote.start()
        else:
            pl.when(here)(pltpu.make_async_copy(src, dst, recv_sem).start)
            pl.when(jnp.logical_not(here))(remote.start)

    def move_kv(phase):
        def body(j, carry):
            device, full, half, col, here = target(phase, j)
            sems = (send_near.at[j] if phase == 0 else send_far.at[0], recv_in.at[row_there, col])
            for i, ref in enumerate((k_ref, v_ref)):
                move(part(ref, full), kv.at[1, row_there, col, 0, i, c], *sems, device, here)
            if phase == 0:
                for i, ref in enumerate((k_ref, v_ref)):
                    move(part(ref, half), kv.at[1, row_there, col, 1, i, c], *sems, device, here)
            return carry

        lax.fori_loop(0, 8, body, 0)

    def move_q(phase):
        def body(j, carry):
            device, full, half, col, here = target(phase, j)
            sems = (send_near.at[j] if phase == 0 else send_far.at[0], recv_q.at[phase])
            move(part(q_ref, full), qb.at[col + 2 * phase, row_there, c], *sems, device, here)
            if phase == 0:
                move(part(q_ref, half), qb.at[2 + col, row_there, c], *sems, device, here)
            return carry

        lax.fori_loop(0, 8, body, 0)

    def sent():
        def body(j, carry):
            pl.when(jnp.logical_not(target(0, j)[4]))(lambda: wait_for(qb.at[pl.ds(0, 3), 0], send_near.at[j]))
            return carry

        lax.fori_loop(0, 8, body, 0)
        wait_for(qb, send_far.at[0])

    def mask_to(j):
        x_t = 2 * c + j
        return (z * ROWS + x_t, 2 * y + core_there), (x_t == x) & (core_there == c)

    def move_mask():
        for j in range(2):
            device, here = mask_to(j)
            move(mask_ref, mb.at[row_there], send_mask.at[j], recv_mask.at[0], device, here)

    move_kv(0)
    move_kv(1)
    move_mask()
    move_q(0)

    def chunk(slot, row, col):
        return kv.at[slot, row, col, 0] if isinstance(col, int) and col >= 2 else kv.at[slot, row, col]

    def pass_on(row, col):
        return [
            (has, pltpu.make_async_remote_copy(
                src_ref=chunk(1, row, col), dst_ref=chunk(slot, row, col),
                send_sem=send_z.at[slot // 2], recv_sem=recv_z.at[slot // 2, row, col],
                device_id=(there, head), device_id_type=MESH,
            ))
            for slot, there, has in ((0, above, has_above), (2, below, has_below))
        ]

    def across(slot, col):
        return pltpu.make_async_remote_copy(
            src_ref=chunk(slot, 1, col), dst_ref=chunk(slot, 2, col),
            send_sem=send_x.at[slot], recv_sem=recv_x.at[slot, col],
            device_id=(seq, 2 * y + 1 - c), device_id_type=MESH,
        )

    def lend(slot):
        return pltpu.make_async_remote_copy(
            src_ref=kv.at[slot, pl.ds(0, 2), 1, 1], dst_ref=kv.at[slot, pl.ds(0, 2), 2, 1],
            send_sem=send_lent.at[slot], recv_sem=recv_lent.at[slot],
            device_id=(seq, (head + 4) % 8), device_id_type=MESH,
        )

    def lend_across(slot):
        return pltpu.make_async_remote_copy(
            src_ref=kv.at[slot, 1, 2, 1], dst_ref=kv.at[slot, 2, 2, 1],
            send_sem=send_lent.at[slot], recv_sem=recv_lent_x.at[slot],
            device_id=(seq, 2 * y + 1 - c), device_id_type=MESH,
        )

    def borrow(slot):
        wait_for(kv.at[slot, pl.ds(0, 2), 2, 1], recv_lent.at[slot])
        lend_across(slot).start()

    def forward(row, col):
        wait_for(chunk(1, row, col), recv_in.at[row, col])
        for has, copy in pass_on(row, col):
            pl.when(has)(copy.start)

    def forward_near(i, carry):
        gap = (x + 4 - i) % 4
        x_from = 2 * c + gap % 2
        col = ((gap + 4 - x_from) % 4) // 2
        row = jnp.where(c == 0, x_from, 3 - x_from)
        forward(row, col)

        @pl.when(row == 1)
        def _():
            across(1, col).start()

        return carry

    @pl.when(z == 0)
    def _():
        pl.semaphore_wait(entered, 1)

    lax.fori_loop(0, 4, forward_near, 0)
    lend(1).start()
    move_q(1)

    def forward_far(col):
        forward(1, col)
        across(1, col).start()
        forward(0, col)

    forward_far(2)
    forward_far(3)

    wait_for(mb, recv_mask.at[0])
    flags = mb[...]
    kept = jnp.where(flags > 0, 1.0, 0.0).astype(F32)
    ahead = [kept[r, i:i + 1, :] for r in range(2) for i in range(4)]
    back = [kept[r, 3 - i:4 - i, :] for r in range(2) for i in range(4)]
    ahead, back = jnp.concatenate(ahead, axis=0), jnp.concatenate(back, axis=0)
    kept = jnp.where(p == 0, ahead, back).astype(BF16)
    lane = lax.broadcasted_iota(jnp.int32, (256, 128), 1)
    tile = lax.broadcasted_iota(jnp.int32, (256, 128), 0)
    slot_of = jnp.where(lane >= 12, 1, 0) + jnp.where(lane >= 24, 1, 0)
    rest = lane - 12 * slot_of
    row_of, col_of = lax.shift_right_logical(rest, 2), lax.bitwise_and(rest, 3)
    row_of = jnp.where(c == 0, row_of, 3 - row_of)
    col_of = jnp.where(p == 0, col_of, 3 - col_of)
    wanted = ((z + slot_of - 1) * ROWS + row_of) * COLS + col_of
    select = jnp.where((wanted == tile) & (lane < 36), 1.0, 0.0).astype(BF16)
    picked = jnp.dot(kept, select, preferred_element_type=F32)
    offset = jnp.where(picked > 0.5, 0.0, MASKED)
    for i in range(36):
        bias[:, i * 128:(i + 1) * 128] = jnp.broadcast_to(offset[:, i:i + 1], (8, 128))

    wait_for(qb.at[pl.ds(0, 4)], recv_q.at[0])
    factor = math.log2(math.e) / math.sqrt(DIM)

    def attend(g, slots, first):
        hd, mid = (0, g) if g < 4 else (1, g - 4)
        lo, hi = max(0, mid - 1), min(3, mid + 1)
        n = hi - lo + 1
        blocks = [(slot, row) for slot in slots for row in range(3)]
        query = qb[PLACE[g]].reshape(2 * TILE, DIM)
        best = [None, None]
        for b, (slot, row) in enumerate(blocks):
            r0 = 0 if row < 2 else 1
            keys = kv[slot, row, lo:hi + 1, hd, 0].reshape(n * TILE, DIM)
            s = lax.dot_general(query[r0 * TILE:], keys, (((1,), (1,)), ((), ())), preferred_element_type=F32)
            for r in range(r0, 2):
                for t in range(n):
                    lanes = (slot * 12 + row * 4 + lo + t) * 128
                    piece = s[(r - r0) * TILE:(r - r0 + 1) * TILE, t * 128:(t + 1) * 128] * factor
                    piece = piece + bias[r * 4 + mid:r * 4 + mid + 1, lanes:lanes + 128]
                    scores[r, b * n + t] = piece
                    best[r] = piece if best[r] is None else jnp.maximum(best[r], piece)
        for r in range(2):
            highest = jnp.broadcast_to(jnp.max(best[r], axis=1, keepdims=True), (TILE, 128))
            if first:
                now, sums = highest, jnp.zeros((TILE, 128), F32)
            else:
                before = top[g, r]
                now = jnp.maximum(before, highest)
                shrink = jnp.exp2(before - now)
                sums = total[g, r] * shrink
                acc[g, r] = acc[g, r] * shrink
            for b, (slot, row) in enumerate(blocks):
                if row == 2 and r == 0:
                    continue
                for t in range(n):
                    weight = jnp.exp2(scores[r, b * n + t] - now)
                    sums = sums + weight
                    probs[r * TILE:(r + 1) * TILE, (b * n + t) * 128:(b * n + t + 1) * 128] = weight.astype(BF16)
            top[g, r], total[g, r] = now, sums
        result = [None, None]
        for b, (slot, row) in enumerate(blocks):
            r0 = 0 if row < 2 else 1
            vals = kv[slot, row, lo:hi + 1, hd, 1].reshape(n * TILE, DIM)
            o = jnp.dot(probs[r0 * TILE:, b * n * 128:(b + 1) * n * 128], vals, preferred_element_type=F32)
            for r in range(r0, 2):
                add = o[(r - r0) * TILE:(r - r0 + 1) * TILE]
                result[r] = add if result[r] is None else result[r] + add
        for r in range(2):
            acc[g, r] = result[r] if first else acc[g, r] + result[r]

    def bring(cols):
        for col in cols:
            for i, (slot, has) in enumerate(((0, has_below), (2, has_above))):
                @pl.when(has)
                def _():
                    wait_for(chunk(slot, 1, col), recv_z.at[i, 1, col])
                    across(slot, col).start()

    sides = ((0, 0, has_below), (1, 2, has_above))

    def on_sides(act):
        for i, slot, has in sides:
            pl.when(has)(lambda: act(i, slot))

    def join(cols):
        def act(i, slot):
            for col in cols:
                wait_for(chunk(slot, 0, col), recv_z.at[i, 0, col])
                wait_for(chunk(slot, 2, col), recv_x.at[slot, col])

        on_sides(act)

    def lend_sides(i, slot):
        wait_for(chunk(slot, 0, 1), recv_z.at[i, 0, 1])
        lend(slot).start()

    for col in (0, 1):
        wait_for(chunk(1, 2, col), recv_x.at[1, col])
    attend(0, (1,), True)
    attend(4, (1,), True)
    bring((0, 1))
    on_sides(lend_sides)
    borrow(1)
    wait_for(chunk(1, 2, 2), recv_x.at[1, 2])
    attend(1, (1,), True)
    wait_for(chunk(1, 2, 3), recv_x.at[1, 3])
    wait_for(qb.at[pl.ds(4, 2)], recv_q.at[1])
    attend(2, (1,), True)
    attend(3, (1,), True)
    wait_for(kv.at[1, 2, 2, 1], recv_lent_x.at[1])
    attend(5, (1,), True)

    def home(g, r):
        mid = g if g < 4 else g - 4
        x_t = jnp.where(c == 0, r, 3 - r)
        y_t = jnp.where(p == 0, mid, 3 - mid)
        return x_t, y_t, (x_t == x) & (y_t == y)

    def send_back(g):
        h = 3 * pair + (2 * p if g < 4 else 1)
        for r in range(2):
            x_t, y_t, mine = home(g, r)
            sem = send_out.at[8] if g in (2, 3) else send_out.at[2 * PLACE[g] + r]
            for half in range(2):
                move(ob.at[g, r, half], part(out_ref, h), sem, recv_out.at[0],
                     (z * ROWS + x_t, 2 * y_t + half), None if g in (2, 3) else mine & (c == half))

    def finish(g):
        attend(g, (0, 2), False)
        for r in range(2):
            whole = jnp.sum(total[g, r], axis=1, keepdims=True)
            ob[g, r] = (acc[g, r] / whole).astype(BF16).reshape(2, HALF, DIM)
        send_back(g)

    on_sides(lambda i, slot: (
        wait_for(chunk(slot, 0, 0), recv_z.at[i, 0, 0]),
        [wait_for(chunk(slot, 2, col), recv_x.at[slot, col]) for col in (0, 1)],
    ) and None)
    finish(0)
    bring((2,))
    finish(4)
    join((2,))
    finish(1)
    bring((3,))
    on_sides(lambda i, slot: borrow(slot))
    join((3,))
    finish(2)
    finish(3)
    on_sides(lambda i, slot: wait_for(kv.at[slot, 2, 2, 1], recv_lent_x.at[slot]))
    finish(5)

    sent()
    for j in range(2):
        device, here = mask_to(j)
        pl.when(jnp.logical_not(here))(lambda: wait_for(mask_ref, send_mask.at[j]))
    wait_for(kv.at[1, 0, pl.ds(0, 3)], send_x.at[1])
    wait_for(kv.at[1, pl.ds(0, 3), 0, 0], send_lent.at[1])

    def sides_sent(i, slot):
        wait_for(kv.at[slot, 0, pl.ds(0, 3)], send_x.at[slot])
        wait_for(kv.at[slot, pl.ds(0, 3), 0, 0], send_lent.at[slot])
        wait_for(kv.at[slot, pl.ds(0, 2), pl.ds(0, 3)], send_z.at[1 - i])

    on_sides(sides_sent)
    for g in (0, 1, 4, 5):
        for r in range(2):
            x_t, y_t, mine = home(g, r)
            sem = send_out.at[2 * PLACE[g] + r]
            pl.when(mine)(lambda: wait_for(ob.at[g, r, 0], sem))
            pl.when(jnp.logical_not(mine))(lambda: wait_for(ob.at[g, r], sem))
    wait_for(ob.at[pl.ds(2, 2)], send_out.at[8])
    wait_for(out_ref, recv_out.at[0])


def body(queries, keys, values, tile_mask):
    dma = pltpu.SemaphoreType.DMA
    return pl.pallas_call(
        kernel,
        out_shape=jax.ShapeDtypeStruct(queries.shape, BF16),
        in_specs=[pl.BlockSpec(memory_space=pl.ANY)] * 4,
        out_specs=pl.BlockSpec(memory_space=pl.ANY),
        scratch_shapes=[
            pltpu.VMEM((3, 3, 4, 2, 2, 2, HALF, DIM), BF16),
            pltpu.VMEM((GROUPS, 2, 2, HALF, DIM), BF16),
            pltpu.VMEM((2, 4, 256), jnp.int32),
            pltpu.VMEM((8, 36 * 128), F32),
            pltpu.VMEM((2, 18, TILE, 128), F32),
            pltpu.VMEM((2 * TILE, 18 * 128), BF16),
            pltpu.VMEM((GROUPS, 2, TILE, 128), F32),
            pltpu.VMEM((GROUPS, 2, TILE, 128), F32),
            pltpu.VMEM((GROUPS, 2, TILE, DIM), F32),
            pltpu.VMEM((GROUPS, 2, 2, HALF, DIM), BF16),
            dma((2, 4)), dma((2, 2, 4)), dma((3, 4)), dma((2,)), dma((1,)), dma((1,)),
            dma((8,)), dma((1,)), dma((2,)), dma((2,)), dma((3,)), dma((9,)),
            pltpu.SemaphoreType.REGULAR,
            dma((3,)), dma((3,)), dma((3,)),
        ],
        compiler_params=pltpu.CompilerParams(
            collective_id=0, has_side_effects=True, vmem_limit_bytes=62 * 1024 * 1024
        ),
        cost_estimate=pl.CostEstimate(flops=2_000_000_000, bytes_accessed=8_000_000, transcendentals=4_000_000),
    )(queries, keys, values, tile_mask)


def solution(mesh):
    placed = (
        P(("seq", "head"), None),
        P(("seq", "head"), None),
        P(("seq", "head"), None),
        P("seq", None),
    )
    return jax.shard_map(
        body, mesh=mesh, in_specs=placed, out_specs=P(("seq", "head"), None), check_vma=False
    )
```

```python
import math

import jax
import jax.numpy as jnp
from jax import lax
from jax.experimental import pallas as pl
from jax.experimental.pallas import tpu as pltpu
from jax.sharding import PartitionSpec as P

MESH = pl.DeviceIdType.MESH
BF16, F32 = jnp.bfloat16, jnp.float32
FRAMES, ROWS, COLS = 16, 4, 4
TILE, HALF, DIM = 128, 64, 128
GROUPS = 6
MASKED = -1e30
PLACE = (0, 1, 4, 5, 2, 3)


def kernel(q_ref, k_ref, v_ref, mask_ref, out_ref, kv, qb, mb, bias, scores, peak, probs, top, total, acc, ob,
           recv_in, recv_z, recv_x, recv_q, recv_mask, recv_out,
           send_near, send_far, send_mask, send_z, send_x, send_out, entered,
           recv_lent, send_lent, recv_lent_x):
    seq, head = lax.axis_index("seq"), lax.axis_index("head")
    z, x = seq // ROWS, seq % ROWS
    y, c = head // 2, head % 2
    p, pair = y // 2, 2 * x + y % 2

    barrier = pltpu.get_barrier_semaphore()
    own = x * 8 + head

    def greet(k, carry):
        other = (own + k) % 32
        pl.semaphore_signal(barrier, inc=1, device_id=(z * ROWS + other // 8, other % 8), device_id_type=MESH)
        return carry

    lax.fori_loop(1, 32, greet, 0)
    above, below = seq + ROWS, seq - ROWS
    has_above, has_below = z < FRAMES - 1, z > 0

    @pl.when(has_above)
    def _():
        pl.semaphore_signal(barrier, inc=1, device_id=(above, head), device_id_type=MESH)

    @pl.when(z > 1)
    def _():
        pl.semaphore_signal(barrier, inc=1, device_id=(below, head), device_id_type=MESH)

    pl.semaphore_wait(barrier, jnp.where(z == 0, 31, jnp.where(has_above, 33, 32)))

    @pl.when(z == 1)
    def _():
        pl.semaphore_signal(entered, inc=1, device_id=(below, head), device_id_type=MESH)

    for slot, has in ((0, has_below), (2, has_above)):
        @pl.when(jnp.logical_not(has))
        def _():
            kv[slot] = jnp.zeros_like(kv[slot])

    row_there = jnp.where(x < 2, x, 3 - x)
    core_there = x // 2
    near = jnp.where(y < 2, y, 3 - y)

    def target(phase, j):
        p_t = (y // 2 + phase) % 2
        x_t = (x + j // 2 + 2 * near) % 4
        yh_t = (y + c + j) % 2
        y_t = 2 * p_t + yh_t
        w_t = 2 * x_t + yh_t
        col = near if phase == 0 else 3 - near
        here = (x_t == x) & (y_t == y) & (core_there == c) if phase == 0 else None
        return (z * ROWS + x_t, 2 * y_t + core_there), 3 * w_t + 2 * p_t, 3 * w_t + 1, col, here

    def part(ref, h):
        return ref.at[:, pl.ds(pl.multiple_of(h * DIM, DIM), DIM)]

    def wait_for(ref, sem):
        pltpu.make_async_copy(ref, ref, sem).wait()

    def move(src, dst, send_sem, recv_sem, device, here=None):
        remote = pltpu.make_async_remote_copy(
            src_ref=src, dst_ref=dst, send_sem=send_sem, recv_sem=recv_sem, device_id=device, device_id_type=MESH
        )
        if here is None:
            remote.start()
        else:
            pl.when(here)(pltpu.make_async_copy(src, dst, recv_sem).start)
            pl.when(jnp.logical_not(here))(remote.start)

    def move_kv(phase):
        def body(j, carry):
            device, full, half, col, here = target(phase, j)
            sems = (send_near.at[j] if phase == 0 else send_far.at[0], recv_in.at[row_there, col])
            for i, ref in enumerate((k_ref, v_ref)):
                move(part(ref, full), kv.at[1, row_there, col, 0, i, c], *sems, device, here)
            if phase == 0:
                for i, ref in enumerate((k_ref, v_ref)):
                    move(part(ref, half), kv.at[1, row_there, col, 1, i, c], *sems, device, here)
            return carry

        lax.fori_loop(0, 8, body, 0)

    def move_q(phase):
        def body(j, carry):
            device, full, half, col, here = target(phase, j)
            sems = (send_near.at[j] if phase == 0 else send_far.at[0], recv_q.at[phase])
            move(part(q_ref, full), qb.at[col + 2 * phase, row_there, c], *sems, device, here)
            if phase == 0:
                move(part(q_ref, half), qb.at[2 + col, row_there, c], *sems, device, here)
            return carry

        lax.fori_loop(0, 8, body, 0)

    def sent():
        def body(j, carry):
            pl.when(jnp.logical_not(target(0, j)[4]))(lambda: wait_for(qb.at[pl.ds(0, 3), 0], send_near.at[j]))
            return carry

        lax.fori_loop(0, 8, body, 0)
        wait_for(qb, send_far.at[0])

    def mask_to(j):
        x_t = 2 * c + j
        return (z * ROWS + x_t, 2 * y + core_there), (x_t == x) & (core_there == c)

    def move_mask():
        for j in range(2):
            device, here = mask_to(j)
            move(mask_ref, mb.at[row_there], send_mask.at[j], recv_mask.at[0], device, here)

    move_kv(0)
    move_kv(1)
    move_mask()
    move_q(0)

    def chunk(slot, row, col):
        return kv.at[slot, row, col, 0] if isinstance(col, int) and col >= 2 else kv.at[slot, row, col]

    def pass_on(row, col):
        return [
            (has, pltpu.make_async_remote_copy(
                src_ref=chunk(1, row, col), dst_ref=chunk(slot, row, col),
                send_sem=send_z.at[slot // 2], recv_sem=recv_z.at[slot // 2, row, col],
                device_id=(there, head), device_id_type=MESH,
            ))
            for slot, there, has in ((0, above, has_above), (2, below, has_below))
        ]

    def across(slot, col):
        return pltpu.make_async_remote_copy(
            src_ref=chunk(slot, 1, col), dst_ref=chunk(slot, 2, col),
            send_sem=send_x.at[slot], recv_sem=recv_x.at[slot, col],
            device_id=(seq, 2 * y + 1 - c), device_id_type=MESH,
        )

    def lend(slot):
        return pltpu.make_async_remote_copy(
            src_ref=kv.at[slot, pl.ds(0, 2), 1, 1], dst_ref=kv.at[slot, pl.ds(0, 2), 2, 1],
            send_sem=send_lent.at[slot], recv_sem=recv_lent.at[slot],
            device_id=(seq, (head + 4) % 8), device_id_type=MESH,
        )

    def lend_across(slot):
        return pltpu.make_async_remote_copy(
            src_ref=kv.at[slot, 1, 2, 1], dst_ref=kv.at[slot, 2, 2, 1],
            send_sem=send_lent.at[slot], recv_sem=recv_lent_x.at[slot],
            device_id=(seq, 2 * y + 1 - c), device_id_type=MESH,
        )

    def borrow(slot):
        wait_for(kv.at[slot, pl.ds(0, 2), 2, 1], recv_lent.at[slot])
        lend_across(slot).start()

    def forward(row, col):
        wait_for(chunk(1, row, col), recv_in.at[row, col])
        for has, copy in pass_on(row, col):
            pl.when(has)(copy.start)

    def forward_near(i, carry):
        gap = (x + 4 - i) % 4
        x_from = 2 * c + gap % 2
        col = ((gap + 4 - x_from) % 4) // 2
        row = jnp.where(c == 0, x_from, 3 - x_from)
        forward(row, col)

        @pl.when(row == 1)
        def _():
            across(1, col).start()

        return carry

    @pl.when(z == 0)
    def _():
        pl.semaphore_wait(entered, 1)

    lax.fori_loop(0, 4, forward_near, 0)
    lend(1).start()
    move_q(1)

    def forward_far(col):
        forward(1, col)
        across(1, col).start()
        forward(0, col)

    forward_far(2)
    forward_far(3)

    wait_for(mb, recv_mask.at[0])
    flags = mb[...]
    kept = jnp.where(flags > 0, 1.0, 0.0).astype(F32)
    ahead = [kept[r, i:i + 1, :] for r in range(2) for i in range(4)]
    back = [kept[r, 3 - i:4 - i, :] for r in range(2) for i in range(4)]
    ahead, back = jnp.concatenate(ahead, axis=0), jnp.concatenate(back, axis=0)
    kept = jnp.where(p == 0, ahead, back).astype(BF16)
    lane = lax.broadcasted_iota(jnp.int32, (256, 128), 1)
    tile = lax.broadcasted_iota(jnp.int32, (256, 128), 0)
    slot_of = jnp.where(lane >= 12, 1, 0) + jnp.where(lane >= 24, 1, 0)
    rest = lane - 12 * slot_of
    row_of, col_of = lax.shift_right_logical(rest, 2), lax.bitwise_and(rest, 3)
    row_of = jnp.where(c == 0, row_of, 3 - row_of)
    col_of = jnp.where(p == 0, col_of, 3 - col_of)
    wanted = ((z + slot_of - 1) * ROWS + row_of) * COLS + col_of
    select = jnp.where((wanted == tile) & (lane < 36), 1.0, 0.0).astype(BF16)
    picked = jnp.dot(kept, select, preferred_element_type=F32)
    offset = jnp.where(picked > 0.5, 0.0, MASKED)
    for i in range(36):
        bias[:, i * 128:(i + 1) * 128] = jnp.broadcast_to(offset[:, i:i + 1], (8, 128))

    wait_for(qb.at[pl.ds(0, 4)], recv_q.at[0])
    factor = math.log2(math.e) / math.sqrt(DIM)

    def layout(g, slots):
        hd, mid = (0, g) if g < 4 else (1, g - 4)
        lo, hi = max(0, mid - 1), min(3, mid + 1)
        return hd, mid, lo, hi, hi - lo + 1, [(slot, row) for slot in slots for row in range(3)]

    def score(g, slots, side):
        hd, mid, lo, hi, n, blocks = layout(g, slots)
        query = qb[PLACE[g]].reshape(2 * TILE, DIM)
        best = [None, None]
        for b, (slot, row) in enumerate(blocks):
            r0 = 0 if row < 2 else 1
            keys = kv[slot, row, lo:hi + 1, hd, 0].reshape(n * TILE, DIM)
            s = lax.dot_general(query[r0 * TILE:], keys, (((1,), (1,)), ((), ())), preferred_element_type=F32)
            for r in range(r0, 2):
                for t in range(n):
                    lanes = (slot * 12 + row * 4 + lo + t) * 128
                    piece = s[(r - r0) * TILE:(r - r0 + 1) * TILE, t * 128:(t + 1) * 128] * factor
                    piece = piece + bias[r * 4 + mid:r * 4 + mid + 1, lanes:lanes + 128]
                    scores[side, r, b * n + t] = piece
                    best[r] = piece if best[r] is None else jnp.maximum(best[r], piece)
            yield
        for r in range(2):
            peak[side, r] = jnp.broadcast_to(jnp.max(best[r], axis=1, keepdims=True), (TILE, 128))
        yield

    def weigh(g, slots, side, first):
        hd, mid, lo, hi, n, blocks = layout(g, slots)
        now, sums, result = [None, None], [None, None], [None, None]
        for r in range(2):
            now[r] = peak[side, r]
            if first:
                sums[r] = jnp.zeros((TILE, 128), F32)
            else:
                before = top[g, r]
                now[r] = jnp.maximum(before, now[r])
                shrink = jnp.exp2(before - now[r])
                sums[r] = total[g, r] * shrink
                acc[g, r] = acc[g, r] * shrink
            top[g, r] = now[r]
        for b, (slot, row) in enumerate(blocks):
            r0 = 0 if row < 2 else 1
            for r in range(r0, 2):
                for t in range(n):
                    weight = jnp.exp2(scores[side, r, b * n + t] - now[r])
                    sums[r] = sums[r] + weight
                    probs[r * TILE:(r + 1) * TILE, (b * n + t) * 128:(b * n + t + 1) * 128] = weight.astype(BF16)
            vals = kv[slot, row, lo:hi + 1, hd, 1].reshape(n * TILE, DIM)
            o = jnp.dot(probs[r0 * TILE:, b * n * 128:(b + 1) * n * 128], vals, preferred_element_type=F32)
            for r in range(r0, 2):
                add = o[(r - r0) * TILE:(r - r0 + 1) * TILE]
                result[r] = add if result[r] is None else result[r] + add
            yield
        for r in range(2):
            total[g, r] = sums[r]
            acc[g, r] = result[r] if first else acc[g, r] + result[r]
        yield

    def together(*parts):
        parts = list(parts)
        while parts:
            for part_ in list(parts):
                if next(part_, StopIteration) is StopIteration:
                    parts.remove(part_)

    def bring(cols):
        for col in cols:
            for i, (slot, has) in enumerate(((0, has_below), (2, has_above))):
                @pl.when(has)
                def _():
                    wait_for(chunk(slot, 1, col), recv_z.at[i, 1, col])
                    across(slot, col).start()

    sides = ((0, 0, has_below), (1, 2, has_above))

    def on_sides(act):
        for i, slot, has in sides:
            pl.when(has)(lambda: act(i, slot))

    def join(cols):
        def act(i, slot):
            for col in cols:
                wait_for(chunk(slot, 0, col), recv_z.at[i, 0, col])
                wait_for(chunk(slot, 2, col), recv_x.at[slot, col])

        on_sides(act)

    def lend_sides(i, slot):
        wait_for(chunk(slot, 0, 1), recv_z.at[i, 0, 1])
        lend(slot).start()

    def home(g, r):
        mid = g if g < 4 else g - 4
        x_t = jnp.where(c == 0, r, 3 - r)
        y_t = jnp.where(p == 0, mid, 3 - mid)
        return x_t, y_t, (x_t == x) & (y_t == y)

    def send_back(g):
        h = 3 * pair + (2 * p if g < 4 else 1)
        for r in range(2):
            x_t, y_t, mine = home(g, r)
            sem = send_out.at[8] if g in (2, 3) else send_out.at[2 * PLACE[g] + r]
            for half in range(2):
                move(ob.at[g, r, half], part(out_ref, h), sem, recv_out.at[0],
                     (z * ROWS + x_t, 2 * y_t + half), None if g in (2, 3) else mine & (c == half))

    def finish(g):
        for r in range(2):
            whole = jnp.sum(total[g, r], axis=1, keepdims=True)
            ob[g, r] = (acc[g, r] / whole).astype(BF16).reshape(2, HALF, DIM)
        send_back(g)

    def before_own(g):
        if g == 0:
            for col in (0, 1):
                wait_for(chunk(1, 2, col), recv_x.at[1, col])
        if g == 1:
            wait_for(chunk(1, 2, 2), recv_x.at[1, 2])
        if g == 2:
            bring((1,))
            on_sides(lend_sides)
            bring((0,))
            borrow(1)
            wait_for(chunk(1, 2, 3), recv_x.at[1, 3])
            wait_for(qb.at[pl.ds(4, 2)], recv_q.at[1])
        if g == 5:
            wait_for(kv.at[1, 2, 2, 1], recv_lent_x.at[1])

    def before_sides(g):
        if g == 0:
            on_sides(lambda i, slot: (
                wait_for(chunk(slot, 0, 0), recv_z.at[i, 0, 0]),
                [wait_for(chunk(slot, 2, col), recv_x.at[slot, col]) for col in (0, 1)],
            ) and None)
        if g == 4:
            bring((2,))
        if g == 1:
            join((2,))
        if g == 2:
            bring((3,))
            join((3,))
        if g == 5:
            on_sides(lambda i, slot: borrow(slot))
            on_sides(lambda i, slot: wait_for(kv.at[slot, 2, 2, 1], recv_lent_x.at[slot]))

    jobs = [(g, (1,), True) for g in (0, 4, 1, 2, 3, 5)] + [(g, (0, 2), False) for g in (0, 4, 1, 2, 3, 5)]
    old = None
    for i, (g, slots, first) in enumerate(jobs + [(None, None, None)]):
        now_running = []
        if g is not None:
            (before_own if first else before_sides)(g)
            now_running.append(score(g, slots, i % 2))
        if old:
            now_running.append(weigh(*old))
        together(*now_running)
        if old and not old[3]:
            finish(old[0])
        old = (g, slots, i % 2, first)

    sent()
    for j in range(2):
        device, here = mask_to(j)
        pl.when(jnp.logical_not(here))(lambda: wait_for(mask_ref, send_mask.at[j]))
    wait_for(kv.at[1, 0, pl.ds(0, 3)], send_x.at[1])
    wait_for(kv.at[1, pl.ds(0, 3), 0, 0], send_lent.at[1])

    def sides_sent(i, slot):
        wait_for(kv.at[slot, 0, pl.ds(0, 3)], send_x.at[slot])
        wait_for(kv.at[slot, pl.ds(0, 3), 0, 0], send_lent.at[slot])
        wait_for(kv.at[slot, pl.ds(0, 2), pl.ds(0, 3)], send_z.at[1 - i])

    on_sides(sides_sent)
    for g in (0, 1, 4, 5):
        for r in range(2):
            x_t, y_t, mine = home(g, r)
            sem = send_out.at[2 * PLACE[g] + r]
            pl.when(mine)(lambda: wait_for(ob.at[g, r, 0], sem))
            pl.when(jnp.logical_not(mine))(lambda: wait_for(ob.at[g, r], sem))
    wait_for(ob.at[pl.ds(2, 2)], send_out.at[8])
    wait_for(out_ref, recv_out.at[0])


def body(queries, keys, values, tile_mask):
    dma = pltpu.SemaphoreType.DMA
    return pl.pallas_call(
        kernel,
        out_shape=jax.ShapeDtypeStruct(queries.shape, BF16),
        in_specs=[pl.BlockSpec(memory_space=pl.ANY)] * 4,
        out_specs=pl.BlockSpec(memory_space=pl.ANY),
        scratch_shapes=[
            pltpu.VMEM((3, 3, 4, 2, 2, 2, HALF, DIM), BF16),
            pltpu.VMEM((GROUPS, 2, 2, HALF, DIM), BF16),
            pltpu.VMEM((2, 4, 256), jnp.int32),
            pltpu.VMEM((8, 36 * 128), F32),
            pltpu.VMEM((2, 2, 18, TILE, 128), F32),
            pltpu.VMEM((2, 2, TILE, 128), F32),
            pltpu.VMEM((2 * TILE, 18 * 128), BF16),
            pltpu.VMEM((GROUPS, 2, TILE, 128), F32),
            pltpu.VMEM((GROUPS, 2, TILE, 128), F32),
            pltpu.VMEM((GROUPS, 2, TILE, DIM), F32),
            pltpu.VMEM((GROUPS, 2, 2, HALF, DIM), BF16),
            dma((2, 4)), dma((2, 2, 4)), dma((3, 4)), dma((2,)), dma((1,)), dma((1,)),
            dma((8,)), dma((1,)), dma((2,)), dma((2,)), dma((3,)), dma((9,)),
            pltpu.SemaphoreType.REGULAR,
            dma((3,)), dma((3,)), dma((3,)),
        ],
        compiler_params=pltpu.CompilerParams(
            collective_id=0, has_side_effects=True, vmem_limit_bytes=62 * 1024 * 1024
        ),
        cost_estimate=pl.CostEstimate(flops=2_000_000_000, bytes_accessed=8_000_000, transcendentals=4_000_000),
    )(queries, keys, values, tile_mask)


def solution(mesh):
    placed = (
        P(("seq", "head"), None),
        P(("seq", "head"), None),
        P(("seq", "head"), None),
        P("seq", None),
    )
    return jax.shard_map(
        body, mesh=mesh, in_specs=placed, out_specs=P(("seq", "head"), None), check_vma=False
    )
```

```python
import math

import jax
import jax.numpy as jnp
from jax import lax
from jax.experimental import pallas as pl
from jax.experimental.pallas import tpu as pltpu
from jax.sharding import PartitionSpec as P

MESH = pl.DeviceIdType.MESH
BF16, F32 = jnp.bfloat16, jnp.float32
FRAMES, ROWS, COLS = 16, 4, 4
TILE, HALF, DIM = 128, 64, 128
GROUPS = 6
MASKED = -1e30
PLACE = (0, 1, 4, 5, 2, 3)


def kernel(q_ref, k_ref, v_ref, mask_ref, out_ref, kv, qb, mb, bias, scores, peak, probs, top, total, acc, ob,
           recv_in, recv_z, recv_x, recv_q, recv_mask, recv_out,
           send_near, send_far, send_mask, send_z, send_x, send_out, entered,
           recv_lent, send_lent, recv_lent_x):
    seq, head = lax.axis_index("seq"), lax.axis_index("head")
    z, x = seq // ROWS, seq % ROWS
    y, c = head // 2, head % 2
    p, pair = y // 2, 2 * x + y % 2

    barrier = pltpu.get_barrier_semaphore()
    own = x * 8 + head

    def greet(k, carry):
        other = lax.bitwise_and(own + k, 31)
        pl.semaphore_signal(barrier, inc=1, device_id=(seq - x + lax.shift_right_logical(other, 3), lax.bitwise_and(other, 7)), device_id_type=MESH)
        return carry

    lax.fori_loop(1, 32, greet, 0)
    above, below = seq + ROWS, seq - ROWS
    has_above, has_below = z < FRAMES - 1, z > 0

    @pl.when(has_above)
    def _():
        pl.semaphore_signal(barrier, inc=1, device_id=(above, head), device_id_type=MESH)

    @pl.when(z > 1)
    def _():
        pl.semaphore_signal(barrier, inc=1, device_id=(below, head), device_id_type=MESH)

    pl.semaphore_wait(barrier, jnp.where(z == 0, 31, jnp.where(has_above, 33, 32)))

    @pl.when(z == 1)
    def _():
        pl.semaphore_signal(entered, inc=1, device_id=(below, head), device_id_type=MESH)

    for slot, has in ((0, has_below), (2, has_above)):
        @pl.when(jnp.logical_not(has))
        def _():
            kv[slot] = jnp.zeros_like(kv[slot])

    row_there = jnp.where(x < 2, x, 3 - x)
    core_there = x // 2
    near = jnp.where(y < 2, y, 3 - y)

    def target(phase, j):
        p_t = (y // 2 + phase) % 2
        x_t = (x + j // 2 + 2 * near) % 4
        yh_t = (y + c + j) % 2
        y_t = 2 * p_t + yh_t
        w_t = 2 * x_t + yh_t
        col = near if phase == 0 else 3 - near
        here = (x_t == x) & (y_t == y) & (core_there == c) if phase == 0 else None
        return (z * ROWS + x_t, 2 * y_t + core_there), 3 * w_t + 2 * p_t, 3 * w_t + 1, col, here

    def part(ref, h):
        return ref.at[:, pl.ds(pl.multiple_of(h * DIM, DIM), DIM)]

    def wait_for(ref, sem):
        pltpu.make_async_copy(ref, ref, sem).wait()

    def move(src, dst, send_sem, recv_sem, device, here=None):
        remote = pltpu.make_async_remote_copy(
            src_ref=src, dst_ref=dst, send_sem=send_sem, recv_sem=recv_sem, device_id=device, device_id_type=MESH
        )
        if here is None:
            remote.start()
        else:
            pl.when(here)(pltpu.make_async_copy(src, dst, recv_sem).start)
            pl.when(jnp.logical_not(here))(remote.start)

    def move_kv(phase):
        def body(j, carry):
            device, full, half, col, here = target(phase, j)
            sems = (send_near.at[j] if phase == 0 else send_far.at[0], recv_in.at[row_there, col])
            for i, ref in enumerate((k_ref, v_ref)):
                move(part(ref, full), kv.at[1, row_there, col, 0, i, c], *sems, device, here)
            if phase == 0:
                for i, ref in enumerate((k_ref, v_ref)):
                    move(part(ref, half), kv.at[1, row_there, col, 1, i, c], *sems, device, here)
            return carry

        lax.fori_loop(0, 8, body, 0)

    def move_q(phase):
        def body(j, carry):
            device, full, half, col, here = target(phase, j)
            sems = (send_near.at[j] if phase == 0 else send_far.at[0], recv_q.at[phase])
            move(part(q_ref, full), qb.at[col + 2 * phase, row_there, c], *sems, device, here)
            if phase == 0:
                move(part(q_ref, half), qb.at[2 + col, row_there, c], *sems, device, here)
            return carry

        lax.fori_loop(0, 8, body, 0)

    def sent():
        def body(j, carry):
            pl.when(jnp.logical_not(target(0, j)[4]))(lambda: wait_for(qb.at[pl.ds(0, 3), 0], send_near.at[j]))
            return carry

        lax.fori_loop(0, 8, body, 0)
        wait_for(qb, send_far.at[0])

    def mask_to(j):
        x_t = 2 * c + j
        return (z * ROWS + x_t, 2 * y + core_there), (x_t == x) & (core_there == c)

    def move_mask():
        for j in range(2):
            device, here = mask_to(j)
            move(mask_ref, mb.at[row_there], send_mask.at[j], recv_mask.at[0], device, here)

    move_kv(0)
    move_kv(1)
    move_mask()
    move_q(0)

    def chunk(slot, row, col):
        return kv.at[slot, row, col, 0] if isinstance(col, int) and col >= 2 else kv.at[slot, row, col]

    def pass_on(row, col):
        return [
            (has, pltpu.make_async_remote_copy(
                src_ref=chunk(1, row, col), dst_ref=chunk(slot, row, col),
                send_sem=send_z.at[slot // 2], recv_sem=recv_z.at[slot // 2, row, col],
                device_id=(there, head), device_id_type=MESH,
            ))
            for slot, there, has in ((0, above, has_above), (2, below, has_below))
        ]

    def across(slot, col):
        return pltpu.make_async_remote_copy(
            src_ref=chunk(slot, 1, col), dst_ref=chunk(slot, 2, col),
            send_sem=send_x.at[slot], recv_sem=recv_x.at[slot, col],
            device_id=(seq, 2 * y + 1 - c), device_id_type=MESH,
        )

    def lend(slot):
        return pltpu.make_async_remote_copy(
            src_ref=kv.at[slot, pl.ds(0, 2), 1, 1], dst_ref=kv.at[slot, pl.ds(0, 2), 2, 1],
            send_sem=send_lent.at[slot], recv_sem=recv_lent.at[slot],
            device_id=(seq, (head + 4) % 8), device_id_type=MESH,
        )

    def lend_across(slot):
        return pltpu.make_async_remote_copy(
            src_ref=kv.at[slot, 1, 2, 1], dst_ref=kv.at[slot, 2, 2, 1],
            send_sem=send_lent.at[slot], recv_sem=recv_lent_x.at[slot],
            device_id=(seq, 2 * y + 1 - c), device_id_type=MESH,
        )

    def borrow(slot):
        wait_for(kv.at[slot, pl.ds(0, 2), 2, 1], recv_lent.at[slot])
        lend_across(slot).start()

    def forward(row, col):
        wait_for(chunk(1, row, col), recv_in.at[row, col])
        for has, copy in pass_on(row, col):
            pl.when(has)(copy.start)

    def forward_near(i, carry):
        gap = (x + 4 - i) % 4
        x_from = 2 * c + gap % 2
        col = ((gap + 4 - x_from) % 4) // 2
        row = jnp.where(c == 0, x_from, 3 - x_from)
        forward(row, col)

        @pl.when(row == 1)
        def _():
            across(1, col).start()

        return carry

    @pl.when(z == 0)
    def _():
        pl.semaphore_wait(entered, 1)

    lax.fori_loop(0, 4, forward_near, 0)
    lend(1).start()
    move_q(1)

    def forward_far(col):
        forward(1, col)
        across(1, col).start()
        forward(0, col)

    forward_far(2)
    forward_far(3)

    wait_for(mb, recv_mask.at[0])
    flags = mb[...]
    kept = jnp.where(flags > 0, 1.0, 0.0).astype(F32)
    ahead = [kept[r, i:i + 1, :] for r in range(2) for i in range(4)]
    back = [kept[r, 3 - i:4 - i, :] for r in range(2) for i in range(4)]
    ahead, back = jnp.concatenate(ahead, axis=0), jnp.concatenate(back, axis=0)
    kept = jnp.where(p == 0, ahead, back).astype(BF16)
    lane = lax.broadcasted_iota(jnp.int32, (256, 128), 1)
    tile = lax.broadcasted_iota(jnp.int32, (256, 128), 0)
    slot_of = jnp.where(lane >= 12, 1, 0) + jnp.where(lane >= 24, 1, 0)
    rest = lane - 12 * slot_of
    row_of, col_of = lax.shift_right_logical(rest, 2), lax.bitwise_and(rest, 3)
    row_of = jnp.where(c == 0, row_of, 3 - row_of)
    col_of = jnp.where(p == 0, col_of, 3 - col_of)
    wanted = ((z + slot_of - 1) * ROWS + row_of) * COLS + col_of
    select = jnp.where((wanted == tile) & (lane < 36), 1.0, 0.0).astype(BF16)
    picked = jnp.dot(kept, select, preferred_element_type=F32)
    offset = jnp.where(picked > 0.5, 0.0, MASKED)
    for i in range(36):
        bias[:, i * 128:(i + 1) * 128] = jnp.broadcast_to(offset[:, i:i + 1], (8, 128))

    wait_for(qb.at[pl.ds(0, 4)], recv_q.at[0])
    factor = math.log2(math.e) / math.sqrt(DIM)

    def layout(g, slots):
        hd, mid = (0, g) if g < 4 else (1, g - 4)
        lo, hi = max(0, mid - 1), min(3, mid + 1)
        return hd, mid, lo, hi, hi - lo + 1, [(slot, row) for slot in slots for row in range(3)]

    def score(g, slots, side):
        hd, mid, lo, hi, n, blocks = layout(g, slots)
        query = qb[PLACE[g]].reshape(2 * TILE, DIM)
        best = [None, None]
        for b, (slot, row) in enumerate(blocks):
            r0 = 0 if row < 2 else 1
            keys = kv[slot, row, lo:hi + 1, hd, 0].reshape(n * TILE, DIM)
            s = lax.dot_general(query[r0 * TILE:], keys, (((1,), (1,)), ((), ())), preferred_element_type=F32)
            for r in range(r0, 2):
                for t in range(n):
                    lanes = (slot * 12 + row * 4 + lo + t) * 128
                    piece = s[(r - r0) * TILE:(r - r0 + 1) * TILE, t * 128:(t + 1) * 128] * factor
                    piece = piece + bias[r * 4 + mid:r * 4 + mid + 1, lanes:lanes + 128]
                    scores[side, r, b * n + t] = piece
                    best[r] = piece if best[r] is None else jnp.maximum(best[r], piece)
            yield
        for r in range(2):
            peak[side, r] = jnp.broadcast_to(jnp.max(best[r], axis=1, keepdims=True), (TILE, 128))
        yield

    def weigh(g, slots, side, first):
        hd, mid, lo, hi, n, blocks = layout(g, slots)
        now, sums, result = [None, None], [None, None], [None, None]
        for r in range(2):
            now[r] = peak[side, r]
            if first:
                sums[r] = jnp.zeros((TILE, 128), F32)
            else:
                before = top[g, r]
                now[r] = jnp.maximum(before, now[r])
                shrink = jnp.exp2(before - now[r])
                sums[r] = total[g, r] * shrink
                acc[g, r] = acc[g, r] * shrink
            top[g, r] = now[r]
        for b, (slot, row) in enumerate(blocks):
            r0 = 0 if row < 2 else 1
            for r in range(r0, 2):
                for t in range(n):
                    weight = jnp.exp2(scores[side, r, b * n + t] - now[r])
                    sums[r] = sums[r] + weight
                    probs[r * TILE:(r + 1) * TILE, (b * n + t) * 128:(b * n + t + 1) * 128] = weight.astype(BF16)
            vals = kv[slot, row, lo:hi + 1, hd, 1].reshape(n * TILE, DIM)
            o = jnp.dot(probs[r0 * TILE:, b * n * 128:(b + 1) * n * 128], vals, preferred_element_type=F32)
            for r in range(r0, 2):
                add = o[(r - r0) * TILE:(r - r0 + 1) * TILE]
                result[r] = add if result[r] is None else result[r] + add
            yield
        for r in range(2):
            total[g, r] = sums[r]
            acc[g, r] = result[r] if first else acc[g, r] + result[r]
        yield

    def together(*parts):
        parts = list(parts)
        while parts:
            for part_ in list(parts):
                if next(part_, StopIteration) is StopIteration:
                    parts.remove(part_)

    def bring(cols):
        for col in cols:
            for i, (slot, has) in enumerate(((0, has_below), (2, has_above))):
                @pl.when(has)
                def _():
                    wait_for(chunk(slot, 1, col), recv_z.at[i, 1, col])
                    across(slot, col).start()

    sides = ((0, 0, has_below), (1, 2, has_above))

    def on_sides(act):
        for i, slot, has in sides:
            pl.when(has)(lambda: act(i, slot))

    def join(cols):
        def act(i, slot):
            for col in cols:
                wait_for(chunk(slot, 0, col), recv_z.at[i, 0, col])
                wait_for(chunk(slot, 2, col), recv_x.at[slot, col])

        on_sides(act)

    def lend_sides(i, slot):
        wait_for(chunk(slot, 0, 1), recv_z.at[i, 0, 1])
        lend(slot).start()

    def home(g, r):
        mid = g if g < 4 else g - 4
        x_t = jnp.where(c == 0, r, 3 - r)
        y_t = jnp.where(p == 0, mid, 3 - mid)
        return x_t, y_t, (x_t == x) & (y_t == y)

    def send_back(g):
        h = 3 * pair + (2 * p if g < 4 else 1)
        for r in range(2):
            x_t, y_t, mine = home(g, r)
            sem = send_out.at[8] if g in (2, 3) else send_out.at[2 * PLACE[g] + r]
            for half in range(2):
                move(ob.at[g, r, half], part(out_ref, h), sem, recv_out.at[0],
                     (z * ROWS + x_t, 2 * y_t + half), None if g in (2, 3) else mine & (c == half))

    def finish(g):
        for r in range(2):
            whole = jnp.sum(total[g, r], axis=1, keepdims=True)
            ob[g, r] = (acc[g, r] / whole).astype(BF16).reshape(2, HALF, DIM)
        send_back(g)

    def before_own(g):
        if g == 0:
            for col in (0, 1):
                wait_for(chunk(1, 2, col), recv_x.at[1, col])
        if g == 1:
            wait_for(chunk(1, 2, 2), recv_x.at[1, 2])
        if g == 2:
            bring((1,))
            on_sides(lend_sides)
            bring((0,))
            borrow(1)
            wait_for(chunk(1, 2, 3), recv_x.at[1, 3])
            wait_for(qb.at[pl.ds(4, 2)], recv_q.at[1])
        if g == 5:
            wait_for(kv.at[1, 2, 2, 1], recv_lent_x.at[1])

    def before_sides(g):
        if g == 0:
            on_sides(lambda i, slot: (
                wait_for(chunk(slot, 0, 0), recv_z.at[i, 0, 0]),
                [wait_for(chunk(slot, 2, col), recv_x.at[slot, col]) for col in (0, 1)],
            ) and None)
        if g == 4:
            bring((2,))
        if g == 1:
            join((2,))
        if g == 2:
            bring((3,))
            join((3,))
        if g == 5:
            on_sides(lambda i, slot: borrow(slot))
            on_sides(lambda i, slot: wait_for(kv.at[slot, 2, 2, 1], recv_lent_x.at[slot]))

    jobs = [(g, (1,), True) for g in (0, 4, 1, 2, 3, 5)] + [(g, (0, 2), False) for g in (0, 4, 1, 2, 3, 5)]
    old = None
    for i, (g, slots, first) in enumerate(jobs + [(None, None, None)]):
        now_running = []
        if g == 5 and not first:
            together(weigh(*old))
            finish(old[0])
            old = None
        if g is not None:
            (before_own if first else before_sides)(g)
            now_running.append(score(g, slots, i % 2))
        if old:
            now_running.append(weigh(*old))
        together(*now_running)
        if old and not old[3]:
            finish(old[0])
        old = (g, slots, i % 2, first)

    sent()
    for j in range(2):
        device, here = mask_to(j)
        pl.when(jnp.logical_not(here))(lambda: wait_for(mask_ref, send_mask.at[j]))
    wait_for(kv.at[1, 0, pl.ds(0, 3)], send_x.at[1])
    wait_for(kv.at[1, pl.ds(0, 3), 0, 0], send_lent.at[1])

    def sides_sent(i, slot):
        wait_for(kv.at[slot, 0, pl.ds(0, 3)], send_x.at[slot])
        wait_for(kv.at[slot, pl.ds(0, 3), 0, 0], send_lent.at[slot])
        wait_for(kv.at[slot, pl.ds(0, 2), pl.ds(0, 3)], send_z.at[1 - i])

    on_sides(sides_sent)
    for g in (0, 1, 4, 5):
        for r in range(2):
            x_t, y_t, mine = home(g, r)
            sem = send_out.at[2 * PLACE[g] + r]
            pl.when(mine)(lambda: wait_for(ob.at[g, r, 0], sem))
            pl.when(jnp.logical_not(mine))(lambda: wait_for(ob.at[g, r], sem))
    wait_for(ob.at[pl.ds(2, 2)], send_out.at[8])
    wait_for(out_ref, recv_out.at[0])


def body(queries, keys, values, tile_mask):
    dma = pltpu.SemaphoreType.DMA
    return pl.pallas_call(
        kernel,
        out_shape=jax.ShapeDtypeStruct(queries.shape, BF16),
        in_specs=[pl.BlockSpec(memory_space=pl.ANY)] * 4,
        out_specs=pl.BlockSpec(memory_space=pl.ANY),
        scratch_shapes=[
            pltpu.VMEM((3, 3, 4, 2, 2, 2, HALF, DIM), BF16),
            pltpu.VMEM((GROUPS, 2, 2, HALF, DIM), BF16),
            pltpu.VMEM((2, 4, 256), jnp.int32),
            pltpu.VMEM((8, 36 * 128), F32),
            pltpu.VMEM((2, 2, 18, TILE, 128), F32),
            pltpu.VMEM((2, 2, TILE, 128), F32),
            pltpu.VMEM((2 * TILE, 18 * 128), BF16),
            pltpu.VMEM((GROUPS, 2, TILE, 128), F32),
            pltpu.VMEM((GROUPS, 2, TILE, 128), F32),
            pltpu.VMEM((GROUPS, 2, TILE, DIM), F32),
            pltpu.VMEM((GROUPS, 2, 2, HALF, DIM), BF16),
            dma((2, 4)), dma((2, 2, 4)), dma((3, 4)), dma((2,)), dma((1,)), dma((1,)),
            dma((8,)), dma((1,)), dma((2,)), dma((2,)), dma((3,)), dma((9,)),
            pltpu.SemaphoreType.REGULAR,
            dma((3,)), dma((3,)), dma((3,)),
        ],
        compiler_params=pltpu.CompilerParams(
            collective_id=0, has_side_effects=True, vmem_limit_bytes=62 * 1024 * 1024
        ),
        cost_estimate=pl.CostEstimate(flops=2_000_000_000, bytes_accessed=8_000_000, transcendentals=4_000_000),
    )(queries, keys, values, tile_mask)


def solution(mesh):
    placed = (
        P(("seq", "head"), None),
        P(("seq", "head"), None),
        P(("seq", "head"), None),
        P("seq", None),
    )
    return jax.shard_map(
        body, mesh=mesh, in_specs=placed, out_specs=P(("seq", "head"), None), check_vma=False
    )
```
